32 devices in a mesh: dp: 2 (over x), ctx: 4 (over z), tensor: 4 (over y, core).
Axes of the slice: x: 2, y: 2, z: 4, core: 2. Of those that a mesh axis runs over, the one named last changes fastest.
Arguments:
- hidden_in: bfloat16 [4, 1024, 768], P('dp', 'ctx'), may hold values from -6 to 6
- cotangent: bfloat16 [4, 1024, 768], P('dp', 'ctx'), may hold values from -6 to 6
- segment_ids: int32 [4, 1024], P('dp'), may hold values from 0 to 2, as said below
- qkv_weight: float32 [3, 768, 768], P(None, ('dp', 'ctx'), 'tensor'), may hold values from -0.21875 to 0.21875
- qkv_first: float32 [3, 768, 768], P(None, ('dp', 'ctx'), 'tensor'), may hold values from -16 to 16
- qkv_second: float32 [3, 768, 768], P(None, ('dp', 'ctx'), 'tensor'), may hold values from 0.53248 to 2.12992
- out_weight: float32 [768, 768], P('tensor', ('dp', 'ctx')), may hold values from -0.875 to 0.875
- out_first: float32 [768, 768], P('tensor', ('dp', 'ctx')), may hold values from -16 to 16
- out_second: float32 [768, 768], P('tensor', ('dp', 'ctx')), may hold values from 0.6144 to 2.4576
- up_weight: float32 [768, 3072], P(('dp', 'ctx'), 'tensor'), may hold values from -0.21875 to 0.21875
- up_first: float32 [768, 3072], P(('dp', 'ctx'), 'tensor'), may hold values from -16 to 16
- up_second: float32 [768, 3072], P(('dp', 'ctx'), 'tensor'), may hold values from 0.53248 to 2.12992
- down_weight: float32 [3072, 768], P('tensor', ('dp', 'ctx')), may hold values from -0.109375 to 0.109375
- down_first: float32 [3072, 768], P('tensor', ('dp', 'ctx')), may hold values from -28 to 28
- down_second: float32 [3072, 768], P('tensor', ('dp', 'ctx')), may hold values from 1.72032 to 6.9632
- vectors: float32 [12, 768], P(None, ('dp', 'ctx')), may hold values from -1.75 to 1.75
- vectors_first: float32 [12, 768], P(None, ('dp', 'ctx')), may hold values from -40 to 40
- vectors_second: float32 [12, 768], P(None, ('dp', 'ctx')), may hold values from 4.096 to 16.384
Outputs:
- block_out: bfloat16 [4, 1024, 768], P('dp', ('ctx', 'tensor'))
- input_grad: float32 [4, 1024, 768], P('dp', ('ctx', 'tensor'))
- qkv_new: float32 [3, 768, 768], P(None, ('dp', 'ctx'), 'tensor')
- qkv_first_new: float32 [3, 768, 768], P(None, ('dp', 'ctx'), 'tensor')
- qkv_second_new: float32 [3, 768, 768], P(None, ('dp', 'ctx'), 'tensor')
- out_new: float32 [768, 768], P('tensor', ('dp', 'ctx'))
- out_first_new: float32 [768, 768], P('tensor', ('dp', 'ctx'))
- out_second_new: float32 [768, 768], P('tensor', ('dp', 'ctx'))
- up_new: float32 [768, 3072], P(('dp', 'ctx'), 'tensor')
- up_first_new: float32 [768, 3072], P(('dp', 'ctx'), 'tensor')
- up_second_new: float32 [768, 3072], P(('dp', 'ctx'), 'tensor')
- down_new: float32 [3072, 768], P('tensor', ('dp', 'ctx'))
- down_first_new: float32 [3072, 768], P('tensor', ('dp', 'ctx'))
- down_second_new: float32 [3072, 768], P('tensor', ('dp', 'ctx'))
- vectors_new: float32 [12, 768], P(None, ('dp', 'ctx'))
- vectors_first_new: float32 [12, 768], P(None, ('dp', 'ctx'))
- vectors_second_new: float32 [12, 768], P(None, ('dp', 'ctx'))
The draws below stay inside these ranges and needn't reach their ends.
Inputs may be any that keep to these rules, and one draw needn't show every extreme that they name: `segment_ids`: each sequence holds three documents numbered 0, 1, 2 in order; document 1 starts at a token index from 64 to 128, and document 2 starts at a token index from 896 to 960.
All inputs are finite; a program needn't handle non-finite values.
Results may differ from the reference program's by a relative error of at most 0.009.
The reference program's roundings to bfloat16 on the way count: a program that leaves them out, or rounds other values in their place, can miss the bound.
Values may be sent and summed in bfloat16 or wider, within the bound.
A program may use at most 128 MiB of HBM per device.

```python
import math
import jax
import jax.numpy as jnp
from jax import lax

D = 768
H = 12
HD = 64
FF = 3072
TOK_CTX = 256
STEP = 10
SEQ = 1024
SEQS = 4
NVEC = 12


def draw_segment_ids(key, part):
    key = jax.random.fold_in(key, 7)
    first_key, second_key = jax.random.split(key)
    opening = jax.random.randint(first_key, (SEQS, 1), TOK_CTX // 4, TOK_CTX // 2 + 1)
    closing = jax.random.randint(second_key, (SEQS, 1), SEQ - TOK_CTX // 2, SEQ - TOK_CTX // 4 + 1)
    places = jnp.arange(SEQ, dtype=jnp.int32)[None, :]
    return (places >= opening).astype(jnp.int32) + (places >= closing).astype(jnp.int32)


def draw_vectors(key, part):
    key = jax.random.fold_in(key, 11)
    noise = jnp.clip(jax.random.normal(key, (NVEC, D), jnp.float32), -3.0, 3.0)
    rows = jnp.arange(NVEC)[:, None]
    gain_rows = (rows == 0) | (rows == 5)
    return jnp.where(gain_rows, 1.0 + 0.25 * noise, 0.3 * noise).astype(jnp.float32)


def block_levels(key, dims, cuts, least, largest):
    level = 1.0
    for axis_at, blocks in cuts:
        draws = jax.random.uniform(jax.random.fold_in(jax.random.fold_in(key, 6), axis_at), (blocks,), jnp.float32, least / len(cuts), largest / len(cuts))
        level = level * jnp.repeat(jnp.exp(draws), dims[axis_at] // blocks).reshape((-1,) + (1,) * (len(dims) - 1 - axis_at))
    return level


def normal_values(stream_key, dims, scale, most, shards=(), held_as=jnp.bfloat16):
    array = jax.random.normal(stream_key, dims, jnp.float32) * scale
    if len(shards) > 0:
        array = block_levels(stream_key, dims, shards, -0.22, 0.18) * array
    return jnp.clip(array, min=-most, max=most).astype(held_as)


def setup_inputs(seed: int = 0) -> dict:
    arg_keys = jax.random.split(jax.random.key(seed), 19)
    return {
        "hidden_in": normal_values(arg_keys[0], (SEQS, SEQ, D), 1.0, 6.0, ((0, 2), (1, 4))),
        "cotangent": normal_values(arg_keys[1], (SEQS, SEQ, D), 1.0, 6.0, ((0, 2), (1, 4))),
        "segment_ids": draw_segment_ids(jax.random.fold_in(arg_keys[18], 71), 0),
        "qkv_weight": normal_values(arg_keys[3], (3, D, D), D ** -0.5, 0.21875, ((1, 8), (2, 4)), jnp.float32),
        "qkv_first": normal_values(arg_keys[4], (3, D, D), (0.04 * (SEQS * SEQ) ** 0.5), 16.0, ((1, 8), (2, 4)), jnp.float32),
        "qkv_second": jnp.clip(jnp.exp(math.log(2.12992) - 1.3862944 * jax.random.uniform(arg_keys[5], (3, D, D), jnp.float32) ** block_levels(arg_keys[5], (3, D, D), ((1, 8), (2, 4)), -0.2, 0.2)), 0.53248, 2.12992),
        "out_weight": normal_values(arg_keys[6], (D, D), (D // 16) ** -0.5, 0.875, ((0, 4), (1, 8)), jnp.float32),
        "out_first": normal_values(arg_keys[7], (D, D), (0.043 * (SEQS * SEQ) ** 0.5), 16.0, ((0, 4), (1, 8)), jnp.float32),
        "out_second": jnp.clip(jnp.exp(math.log(2.4576) - 1.3862944 * jax.random.uniform(arg_keys[8], (D, D), jnp.float32) ** block_levels(arg_keys[8], (D, D), ((0, 4), (1, 8)), -0.2, 0.2)), 0.6144, 2.4576),
        "up_weight": normal_values(arg_keys[9], (D, FF), D ** -0.5, 0.21875, ((0, 8), (1, 4)), jnp.float32),
        "up_first": normal_values(arg_keys[10], (D, FF), (0.04 * (SEQS * SEQ) ** 0.5), 16.0, ((0, 8), (1, 4)), jnp.float32),
        "up_second": jnp.clip(jnp.exp(math.log(2.12992) - 1.3862944 * jax.random.uniform(arg_keys[11], (D, FF), jnp.float32) ** block_levels(arg_keys[11], (D, FF), ((0, 8), (1, 4)), -0.2, 0.2)), 0.53248, 2.12992),
        "down_weight": normal_values(arg_keys[12], (FF, D), FF ** -0.5, 0.109375, ((0, 4), (1, 8)), jnp.float32),
        "down_first": normal_values(arg_keys[13], (FF, D), (0.0715 * (SEQS * SEQ) ** 0.5), 28.0, ((0, 4), (1, 8)), jnp.float32),
        "down_second": jnp.clip(jnp.exp(math.log(6.9632) - 1.39812884 * jax.random.uniform(arg_keys[14], (FF, D), jnp.float32) ** block_levels(arg_keys[14], (FF, D), ((0, 4), (1, 8)), -0.2, 0.2)), 1.72032, 6.9632),
        "vectors": draw_vectors(jax.random.fold_in(arg_keys[18], 71), 0),
        "vectors_first": normal_values(arg_keys[16], (NVEC, D), (0.11 * (SEQS * SEQ) ** 0.5), 40.0, ((1, 8),), jnp.float32),
        "vectors_second": jnp.clip(jnp.exp(math.log(16.384) - 1.3862944 * jax.random.uniform(arg_keys[17], (NVEC, D), jnp.float32) ** block_levels(arg_keys[17], (NVEC, D), ((1, 8),), -0.2, 0.2)), 4.096, 16.384),
    }


@jax.custom_vjp
def low(v):
    return lax.optimization_barrier(v.astype(jnp.bfloat16)).astype(jnp.float32)

@jax.custom_vjp
def low_back(v):
    return v

def low_keep(v):
    return (low(v), None)

def low_pass(kept, grad):
    return (grad,)

def back_keep(v):
    return (v, None)

def back_low(kept, grad):
    return (low(grad),)
low.defvjp(low_keep, low_pass)
low_back.defvjp(back_keep, back_low)
norm_eps = 1e-05
beta_first = 0.9
beta_second = 0.999
adam_eps = 1e-08
weight_decay = 0.01
rate_qkv = 0.05
rate_out = 0.2
rate_up = 0.05
rate_down = 0.025
rate_vectors = 0.3
highest = lax.Precision.HIGHEST

def product(left, right):
    return jnp.dot(left, right, precision=highest, preferred_element_type=jnp.float32)

def normed(values, gain, shift):
    centre = values - lax.optimization_barrier(jnp.mean(values, axis=-1, keepdims=True))
    spread = lax.optimization_barrier(jnp.mean(centre * centre, axis=-1, keepdims=True))
    return centre * lax.rsqrt(spread + norm_eps) * gain + shift

def attend(query, keys, values, segment):
    length = query.shape[0]
    places = jnp.arange(length)
    allowed = (places[:, None] >= places[None, :]) & (segment[:, None] == segment[None, :])

    def one_head(head_args):
        head_query, head_keys, head_values = head_args
        scores = low_back(product(head_query, head_keys.T)) * HD ** (-0.5)
        scores = jnp.where(allowed, scores, -1e+30)
        highest_score = lax.optimization_barrier(jnp.max(scores, axis=-1, keepdims=True))
        weights = jnp.exp(scores - highest_score)
        probs_full = weights / lax.optimization_barrier(jnp.sum(weights, axis=-1, keepdims=True))
        return product(low(probs_full), head_values)

    def by_head(matrix):
        return matrix.reshape(length, H, HD).transpose(1, 0, 2)
    results = lax.map(jax.checkpoint(one_head), (by_head(query), by_head(keys), by_head(values)))
    return results.transpose(1, 0, 2).reshape(length, H * HD)

def forward(inputs, qkv_weight, out_weight, up_weight, down_weight, vectors, segment):
    table = low(vectors)
    first_norm = low(normed(inputs, table[0], table[1]))
    projections = low(qkv_weight)
    query = low(low_back(product(first_norm, projections[0])) + table[2])
    keys = low(low_back(product(first_norm, projections[1])))
    values = low(low_back(product(first_norm, projections[2])) + table[3])
    mixed = low_back(low(attend(query, keys, values, segment)))
    middle = inputs + low_back(product(mixed, low(out_weight))) + table[4]
    second_norm = low(normed(middle, table[5], table[6]))
    hidden = low_back(product(second_norm, low(up_weight))) + table[8:].reshape(FF)
    active = low(jax.nn.gelu(hidden))
    return middle + low_back(product(active, low(down_weight))) + table[7]

def adamw(weight, first, second, grad, rate, decay):
    first_new = beta_first * first + (1.0 - beta_first) * grad
    second_new = beta_second * second + (1.0 - beta_second) * grad * grad
    fix_first = 1.0 - beta_first ** STEP
    fix_second = 1.0 - beta_second ** STEP
    update = first_new / fix_first / (jnp.sqrt(second_new / fix_second) + adam_eps)
    return (weight - rate * (update + decay * weight), first_new, second_new)

def reference(hidden_in, cotangent, segment_ids, qkv_weight, qkv_first, qkv_second, out_weight, out_first, out_second, up_weight, up_first, up_second, down_weight, down_first, down_second, vectors, vectors_first, vectors_second):
    params = (qkv_weight, out_weight, up_weight, down_weight, vectors)

    def one_sequence(totals, items):
        inputs, back, segment = items

        def run(values, weights):
            return forward(values, weights[0], weights[1], weights[2], weights[3], weights[4], segment)
        result, pull = jax.vjp(run, inputs.astype(jnp.float32), params)
        in_grad, weight_grads = pull(back.astype(jnp.float32))
        totals = jax.tree.map(lambda left, right: left + right, totals, weight_grads)
        return (totals, (result.astype(jnp.bfloat16), in_grad))
    start = jax.tree.map(jnp.zeros_like, params)
    totals, (block_out, input_grad) = lax.scan(one_sequence, start, (hidden_in, cotangent, segment_ids))
    qkv_new, qkv_first_new, qkv_second_new = adamw(qkv_weight, qkv_first, qkv_second, totals[0], rate_qkv, weight_decay)
    out_new, out_first_new, out_second_new = adamw(out_weight, out_first, out_second, totals[1], rate_out, weight_decay)
    up_new, up_first_new, up_second_new = adamw(up_weight, up_first, up_second, totals[2], rate_up, weight_decay)
    down_new, down_first_new, down_second_new = adamw(down_weight, down_first, down_second, totals[3], rate_down, weight_decay)
    vectors_new, vectors_first_new, vectors_second_new = adamw(vectors, vectors_first, vectors_second, totals[4], rate_vectors, 0.0)
    return (block_out, input_grad, qkv_new, qkv_first_new, qkv_second_new, out_new, out_first_new, out_second_new, up_new, up_first_new, up_second_new, down_new, down_first_new, down_second_new, vectors_new, vectors_first_new, vectors_second_new)
```

```python
import jax
import jax.numpy as jnp
from jax import lax
from jax.sharding import PartitionSpec as P

HD = 64
STEP = 10

norm_eps = 1e-05
beta_first = 0.9
beta_second = 0.999
adam_eps = 1e-08
weight_decay = 0.01
rate_qkv = 0.05
rate_out = 0.2
rate_up = 0.05
rate_down = 0.025
rate_vectors = 0.3

LOW = jnp.bfloat16
F32 = jnp.float32


def dot(left, right, left_dim, right_dim):
    return lax.dot_general(
        left, right, (((left_dim,), (right_dim,)), ((), ())), preferred_element_type=F32
    )


def unit_norm(values):
    centre = values - jnp.mean(values, axis=-1, keepdims=True)
    scale = lax.rsqrt(jnp.mean(centre * centre, axis=-1, keepdims=True) + norm_eps)
    return centre * scale, scale


def norm_back(grad, gain, unit, scale):
    inner = grad * gain
    return scale * (
        inner
        - jnp.mean(inner, axis=-1, keepdims=True)
        - unit * jnp.mean(inner * unit, axis=-1, keepdims=True)
    )


def adamw(weight, first, second, grad, rate, decay):
    first_new = beta_first * first + (1.0 - beta_first) * grad
    second_new = beta_second * second + (1.0 - beta_second) * grad * grad
    fix_first = 1.0 - beta_first**STEP
    fix_second = 1.0 - beta_second**STEP
    update = first_new / fix_first / (jnp.sqrt(second_new / fix_second) + adam_eps)
    return (weight - rate * (update + decay * weight), first_new, second_new)


def gather_weights(shard):
    return lax.all_gather(shard, ("dp", "ctx"), axis=0, tiled=True)


def scatter_grads(grads):
    return lax.psum_scatter(grads, ("dp", "ctx"), scatter_dimension=0, tiled=True)


def gather_ctx(values):
    return lax.all_gather(values, "ctx", axis=1, tiled=True)


def scatter_ctx(values):
    return lax.psum_scatter(values, "ctx", scatter_dimension=1, tiled=True)


def gather_tensor(values):
    return lax.all_gather(values, "tensor", axis=1, tiled=True)


def scatter_tensor(values):
    return lax.psum_scatter(values, "tensor", scatter_dimension=1, tiled=True)


def my_rows(values):
    part = values.shape[1] // lax.axis_size("tensor")
    return lax.dynamic_slice_in_dim(values, lax.axis_index("tensor") * part, part, 1)


def allowed_pairs(segment, tokens):
    ctx_index = lax.axis_index("ctx")
    key_places = jnp.arange(segment.shape[1], dtype=jnp.int32)
    query_places = ctx_index * tokens + jnp.arange(tokens, dtype=jnp.int32)
    query_segment = lax.dynamic_slice_in_dim(segment, ctx_index * tokens, tokens, 1)
    return (query_places[None, :, None] >= key_places[None, None, :]) & (
        query_segment[:, :, None] == segment[:, None, :]
    )


def heads_of(values):
    batch, tokens, width = values.shape
    return values.reshape(batch, tokens, width // HD, HD)


def attend(query, keys, values, allowed):
    scores = jnp.einsum(
        "bqhd,bkhd->bhqk", heads_of(query), heads_of(keys), preferred_element_type=F32
    ) * HD ** (-0.5)
    scores = jnp.where(allowed[:, None], scores, -1e30)
    weights = jnp.exp(scores - jnp.max(scores, axis=-1, keepdims=True))
    probs = weights / jnp.sum(weights, axis=-1, keepdims=True)
    mixed = jnp.einsum(
        "bhqk,bkhd->bqhd", probs.astype(LOW), heads_of(values), preferred_element_type=F32
    )
    return mixed.reshape(query.shape).astype(LOW), probs


def attend_back(mixed_grad, query, keys, values, probs):
    grad_heads = heads_of(mixed_grad)
    prob_grad = jnp.einsum(
        "bqhd,bkhd->bhqk", grad_heads, heads_of(values), preferred_element_type=F32
    )
    row_delta = jnp.sum(prob_grad * probs, axis=-1, keepdims=True)
    score_grad = (probs * (prob_grad - row_delta) * HD ** (-0.5)).astype(LOW)
    query_grad = jnp.einsum(
        "bhqk,bkhd->bqhd", score_grad, heads_of(keys), preferred_element_type=F32
    ).reshape(query.shape)
    key_grad = jnp.einsum(
        "bhqk,bqhd->bkhd", score_grad, heads_of(query), preferred_element_type=F32
    ).reshape(keys.shape)
    value_grad = jnp.einsum(
        "bhqk,bqhd->bkhd", probs.astype(LOW), grad_heads, preferred_element_type=F32
    ).reshape(keys.shape)
    return query_grad, key_grad, value_grad


def on_device(
    hidden_in,
    cotangent,
    segment_ids,
    qkv_weight,
    qkv_first,
    qkv_second,
    out_weight,
    out_first,
    out_second,
    up_weight,
    up_first,
    up_second,
    down_weight,
    down_first,
    down_second,
    vectors,
    vectors_first,
    vectors_second,
):
    batch, tokens, model = hidden_in.shape
    width = qkv_weight.shape[2]
    units = up_weight.shape[1]
    rows_all = batch * tokens
    tensor_index = lax.axis_index("tensor")

    attn_shard = jnp.concatenate(
        [qkv_weight[0], qkv_weight[1], qkv_weight[2]], axis=1
    ).astype(LOW)
    rest_shard = jnp.concatenate([out_weight.T, up_weight, down_weight.T], axis=1).astype(LOW)
    table = lax.all_gather(
        vectors.astype(LOW), ("dp", "ctx"), axis=1, tiled=True
    ).astype(F32)
    proj = gather_weights(attn_shard)
    rest = gather_weights(rest_shard)
    out_turned = rest[:, :width]
    up = rest[:, width : width + units]
    down_turned = rest[:, width + units :]

    inputs = hidden_in.astype(F32)
    unit_first, scale_first = unit_norm(inputs)
    first_norm = (unit_first * table[0] + table[1]).astype(LOW).reshape(rows_all, model)
    projected = dot(first_norm, proj, 1, 0)
    query_bias = lax.dynamic_slice_in_dim(table[2], tensor_index * width, width)
    value_bias = lax.dynamic_slice_in_dim(table[3], tensor_index * width, width)
    query = (projected[:, :width] + query_bias).astype(LOW).reshape(batch, tokens, width)
    local_kv = (
        jnp.concatenate([projected[:, width : 2 * width], projected[:, 2 * width :] + value_bias], axis=1)
        .astype(LOW)
        .reshape(batch, tokens, 2 * width)
    )
    all_kv = gather_ctx(local_kv)
    keys, values = all_kv[..., :width], all_kv[..., width:]
    allowed = allowed_pairs(segment_ids, tokens)
    mixed, probs = attend(query, keys, values, allowed)
    mixed = mixed.reshape(rows_all, width)

    attn_part = dot(mixed, out_turned, 1, 1).astype(LOW).reshape(batch, tokens, model)
    middle = my_rows(inputs) + scatter_tensor(attn_part).astype(F32) + table[4]
    unit_second, scale_second = unit_norm(middle)
    second_norm = gather_tensor((unit_second * table[5] + table[6]).astype(LOW))
    second_norm = second_norm.reshape(rows_all, model)
    unit_bias = lax.dynamic_slice_in_dim(table[8:].reshape(-1), tensor_index * units, units)
    hidden = dot(second_norm, up, 1, 0) + unit_bias
    gelu_value, gelu_pull = jax.vjp(jax.nn.gelu, hidden)
    active = gelu_value.astype(LOW)
    down_part = dot(active, down_turned, 1, 1).astype(LOW).reshape(batch, tokens, model)
    result = (middle + scatter_tensor(down_part).astype(F32) + table[7]).astype(LOW)

    back = cotangent.reshape(rows_all, model)
    back_rows = my_rows(cotangent).astype(F32)
    hidden_grad = gelu_pull(dot(back, down_turned, 1, 0))[0]
    hidden_low = hidden_grad.astype(LOW)
    second_part = dot(hidden_low, up, 1, 1).astype(LOW).reshape(batch, tokens, model)
    second_grad = scatter_tensor(second_part).astype(F32)
    grad_down = dot(back, active, 0, 0)
    grad_up = dot(second_norm, hidden_low, 0, 0)
    late_sum = scatter_grads(jnp.concatenate([grad_up, grad_down], axis=1).astype(LOW))

    middle_grad = back_rows + norm_back(second_grad, table[5], unit_second, scale_second)
    middle_low = gather_tensor(middle_grad.astype(LOW)).reshape(rows_all, model)
    mixed_grad = dot(middle_low, out_turned, 1, 0).astype(LOW).reshape(batch, tokens, width)
    query_grad, key_part, value_part = attend_back(mixed_grad, query, keys, values, probs)
    kv_grad = scatter_ctx(jnp.concatenate([key_part, value_part], axis=2).astype(LOW))
    grad_out = dot(middle_low, mixed, 0, 0)
    stacked = jnp.concatenate([query_grad.astype(LOW), kv_grad], axis=2).reshape(
        rows_all, 3 * width
    )
    first_part = dot(stacked, proj, 1, 1).astype(LOW).reshape(batch, tokens, model)
    first_grad = scatter_tensor(first_part).astype(F32)
    grad_qkv = dot(first_norm, stacked, 0, 0)
    early_sum = scatter_grads(jnp.concatenate([grad_qkv, grad_out], axis=1).astype(LOW))
    my_unit, my_scale = my_rows(unit_first), my_rows(scale_first)
    input_grad = middle_grad + norm_back(first_grad, table[0], my_unit, my_scale)

    def total(values):
        return jnp.sum(values, axis=(0, 1))

    owned = jnp.zeros((vectors.shape[0] * model,), F32)
    owned = lax.dynamic_update_slice(
        owned, total(query_grad), (2 * model + tensor_index * width,)
    )
    owned = lax.dynamic_update_slice(
        owned, total(value_part), (3 * model + tensor_index * width,)
    )
    owned = lax.dynamic_update_slice(
        owned, jnp.sum(hidden_grad, axis=0), (8 * model + tensor_index * units,)
    )
    zero = jnp.zeros((model,), F32)
    rows = jnp.stack(
        [total(first_grad * my_unit), total(first_grad), zero, zero]
        + [total(middle_grad), total(second_grad * unit_second)]
        + [total(second_grad), total(back_rows)]
        + [zero] * (vectors.shape[0] - 8)
    )
    grad_table = lax.psum(owned.reshape(rows.shape) + rows, ("dp", "ctx", "tensor"))
    part = vectors.shape[1]
    grad_vectors = lax.dynamic_slice_in_dim(
        grad_table,
        (lax.axis_index("dp") * lax.axis_size("ctx") + lax.axis_index("ctx")) * part,
        part,
        1,
    )

    early_sum = early_sum.astype(F32)
    late_sum = late_sum.astype(F32)
    qkv_sum = jnp.stack([early_sum[:, place * width : (place + 1) * width] for place in range(3)])
    out_sum = early_sum[:, 3 * width :].T
    up_sum = late_sum[:, :units]
    down_sum = late_sum[:, units:].T
    return (
        result,
        input_grad,
        *adamw(qkv_weight, qkv_first, qkv_second, qkv_sum, rate_qkv, weight_decay),
        *adamw(out_weight, out_first, out_second, out_sum, rate_out, weight_decay),
        *adamw(up_weight, up_first, up_second, up_sum, rate_up, weight_decay),
        *adamw(down_weight, down_first, down_second, down_sum, rate_down, weight_decay),
        *adamw(vectors, vectors_first, vectors_second, grad_vectors, rate_vectors, 0.0),
    )


def solution(mesh):
    tokens = P("dp", "ctx", None)
    shares = P("dp", ("ctx", "tensor"), None)
    by_row = P(("dp", "ctx"), "tensor")
    by_column = P("tensor", ("dp", "ctx"))
    stacked = P(None, ("dp", "ctx"), "tensor")
    narrow = P(None, ("dp", "ctx"))
    states = (stacked,) * 3 + (by_column,) * 3 + (by_row,) * 3 + (by_column,) * 3 + (narrow,) * 3
    return jax.shard_map(
        on_device,
        mesh=mesh,
        in_specs=(tokens, tokens, P("dp", None)) + states,
        out_specs=(shares, shares) + states,
        check_vma=False,
    )
```

```python
import jax
import jax.numpy as jnp
from jax import lax
from jax.experimental import pallas as pl
from jax.experimental.pallas import tpu as pltpu
from jax.sharding import PartitionSpec as P

HD = 64
STEP = 10

norm_eps = 1e-05
beta_first = 0.9
beta_second = 0.999
adam_eps = 1e-08
weight_decay = 0.01
rate_qkv = 0.05
rate_out = 0.2
rate_up = 0.05
rate_down = 0.025
rate_vectors = 0.3

LOW = jnp.bfloat16
F32 = jnp.float32


def dot(left, right, left_dim, right_dim):
    return lax.dot_general(
        left, right, (((left_dim,), (right_dim,)), ((), ())), preferred_element_type=F32
    )


def unit_norm(values):
    centre = values - jnp.mean(values, axis=-1, keepdims=True)
    scale = lax.rsqrt(jnp.mean(centre * centre, axis=-1, keepdims=True) + norm_eps)
    return centre * scale, scale


def norm_back(grad, gain, unit, scale):
    inner = grad * gain
    return scale * (
        inner
        - jnp.mean(inner, axis=-1, keepdims=True)
        - unit * jnp.mean(inner * unit, axis=-1, keepdims=True)
    )


def adamw(weight, first, second, grad, rate, decay):
    first_new = beta_first * first + (1.0 - beta_first) * grad
    second_new = beta_second * second + (1.0 - beta_second) * grad * grad
    fix_first = 1.0 - beta_first**STEP
    fix_second = 1.0 - beta_second**STEP
    update = first_new / fix_first / (jnp.sqrt(second_new / fix_second) + adam_eps)
    return (weight - rate * (update + decay * weight), first_new, second_new)


def whole(count):
    return [pl.BlockSpec(memory_space=pltpu.VMEM)] * count


def params(number):
    return pltpu.CompilerParams(
        collective_id=number, has_side_effects=True, vmem_limit_bytes=48 * 2**20
    )


def place(axis, step):
    size = lax.axis_size(axis)
    return lax.rem(lax.axis_index(axis) + step + size, size)


def push(source, target, sends, receives, device):
    copy = pltpu.make_async_remote_copy(
        src_ref=source,
        dst_ref=target,
        send_sem=sends,
        recv_sem=receives,
        device_id=device,
        device_id_type=pl.DeviceIdType.MESH,
    )
    copy.start()
    return copy


def greet(axes):
    barrier = pltpu.get_barrier_semaphore()
    count = 0
    for axis in axes:
        for step in range(1, lax.axis_size(axis)):
            pl.semaphore_signal(
                barrier,
                inc=1,
                device_id={axis: place(axis, step)},
                device_id_type=pl.DeviceIdType.MESH,
            )
            count += 1
    pl.semaphore_wait(barrier, count)


def weights_kernel(shard, small, out, small_out, zs, zr, xs, xr, szs, szr, sxs, sxr):
    groups, rows = lax.axis_size("dp"), lax.axis_size("ctx")
    me_dp, me_ctx = lax.axis_index("dp"), lax.axis_index("ctx")
    greet(("dp", "ctx"))
    waits = []
    along = []
    for source, target, sends, receives in ((small, small_out, szs, szr), (shard, out, zs, zr)):
        for step in range(1, rows):
            along.append(
                push(
                    source,
                    target.at[me_dp, me_ctx],
                    sends.at[step - 1],
                    receives.at[step - 1],
                    {"ctx": place("ctx", step)},
                )
            )
    across = []
    arrived = iter(along)
    for source, target, sends, receives in ((small, small_out, sxs, sxr), (shard, out, xs, xr)):
        target[me_dp, me_ctx] = source[...]
        for step in range(rows):
            owner = place("ctx", -step)
            if step > 0:
                next(arrived).wait_recv()
            block = source if step == 0 else target.at[me_dp, owner]
            for far in range(1, groups):
                across.append(
                    push(
                        block,
                        target.at[me_dp, owner],
                        sends.at[step, far - 1],
                        receives.at[step, far - 1],
                        {"dp": place("dp", far)},
                    )
                )
    for copy in across:
        copy.wait_recv()
    for copy in along + across:
        copy.wait_send()


def gather_weights(shard, small):
    groups, rows = lax.axis_size("dp"), lax.axis_size("ctx")
    dma = pltpu.SemaphoreType.DMA
    one = [dma((max(rows - 1, 1),))] * 2 + [dma((rows, max(groups - 1, 1)))] * 2
    return pl.pallas_call(
        weights_kernel,
        out_shape=(
            jax.ShapeDtypeStruct((groups, rows) + shard.shape, shard.dtype),
            jax.ShapeDtypeStruct((groups, rows) + small.shape, small.dtype),
        ),
        in_specs=whole(2),
        out_specs=tuple(whole(2)),
        scratch_shapes=one + one,
        compiler_params=params(1),
    )(shard, small)


def gather_ctx_kernel(local, out, sends, receives):
    rows, tokens = lax.axis_size("ctx"), local.shape[1]
    start = pl.multiple_of(lax.axis_index("ctx") * tokens, tokens)
    greet(("ctx",))
    copies = [
        push(
            local,
            out.at[:, pl.ds(start, tokens), :],
            sends.at[step - 1],
            receives.at[step - 1],
            {"ctx": place("ctx", step)},
        )
        for step in range(1, rows)
    ]
    out[:, pl.ds(start, tokens), :] = local[...]
    for copy in copies:
        copy.wait()


def gather_ctx(local):
    rows = lax.axis_size("ctx")
    batch, tokens, width = local.shape
    return pl.pallas_call(
        gather_ctx_kernel,
        out_shape=jax.ShapeDtypeStruct((batch, rows * tokens, width), local.dtype),
        in_specs=whole(1),
        out_specs=whole(1)[0],
        scratch_shapes=[pltpu.SemaphoreType.DMA((rows - 1,))] * 2,
        compiler_params=params(2),
    )(local)


def scatter_ctx_kernel(parts, out, landing, sends, receives):
    rows, tokens = lax.axis_size("ctx"), out.shape[1]
    greet(("ctx",))
    copies = []
    for step in range(1, rows):
        peer = place("ctx", step)
        copies.append(
            push(
                parts.at[:, pl.ds(pl.multiple_of(peer * tokens, tokens), tokens), :],
                landing.at[step - 1],
                sends.at[step - 1],
                receives.at[step - 1],
                {"ctx": peer},
            )
        )
    start = pl.multiple_of(lax.axis_index("ctx") * tokens, tokens)
    for copy in copies:
        copy.wait()
    total = parts[:, pl.ds(start, tokens), :].astype(F32)
    for step in range(1, rows):
        total = total + landing[step - 1].astype(F32)
    out[...] = total.astype(LOW)


def scatter_ctx(parts):
    rows = lax.axis_size("ctx")
    batch, length, width = parts.shape
    shape = (batch, length // rows, width)
    return pl.pallas_call(
        scatter_ctx_kernel,
        out_shape=jax.ShapeDtypeStruct(shape, LOW),
        in_specs=whole(1),
        out_specs=whole(1)[0],
        scratch_shapes=[pltpu.VMEM((rows - 1,) + shape, LOW)]
        + [pltpu.SemaphoreType.DMA((rows - 1,))] * 2,
        compiler_params=params(3),
    )(parts)


def start_shares(parts, landing, sends, receives):
    share = landing.shape[2]
    copies = []
    for step in range(1, lax.axis_size("tensor")):
        peer = place("tensor", step)
        copies.append(
            push(
                parts.at[:, pl.ds(pl.multiple_of(peer * share, share), share), :],
                landing.at[step - 1],
                sends.at[step - 1],
                receives.at[step - 1],
                {"tensor": peer},
            )
        )
    return copies


def sum_shares(parts, landing, start):
    total = parts[:, pl.ds(start, landing.shape[2]), :].astype(F32)
    for step in range(landing.shape[0]):
        total = total + landing[step].astype(F32)
    return total


def spread_shares(out, start, share, sends, receives):
    copies = []
    for step in range(1, lax.axis_size("tensor")):
        mine = out.at[:, pl.ds(start, share), :]
        copies.append(
            push(
                mine, mine, sends.at[step - 1], receives.at[step - 1], {"tensor": place("tensor", step)}
            )
        )
    return copies


def forward_share_kernel(parts, inputs, table, out, middle, landing, s0, r0, s1, r1):
    share = middle.shape[1]
    start = pl.multiple_of(lax.axis_index("tensor") * share, share)
    greet(("tensor",))
    copies = start_shares(parts, landing, s0, r0)
    for copy in copies:
        copy.wait()
    total = sum_shares(parts, landing, start)
    values = inputs[:, pl.ds(start, share), :].astype(F32) + total + table[4:5][None]
    middle[...] = values
    unit, scale = unit_norm(values)
    out[:, pl.ds(start, share), :] = (unit * table[5:6][None] + table[6:7][None]).astype(LOW)
    for copy in spread_shares(out, start, share, s1, r1):
        copy.wait()


def backward_share_kernel(parts, back, middle, table, out, grad, sums, landing, s0, r0, s1, r1):
    share = middle.shape[1]
    start = pl.multiple_of(lax.axis_index("tensor") * share, share)
    greet(("tensor",))
    copies = start_shares(parts, landing, s0, r0)
    back_rows = back[:, pl.ds(start, share), :].astype(F32)
    unit, scale = unit_norm(middle[...])
    for copy in copies:
        copy.wait()
    total = sum_shares(parts, landing, start)
    values = back_rows + norm_back(total, table[5:6][None], unit, scale)
    grad[...] = values
    out[:, pl.ds(start, share), :] = values.astype(LOW)
    copies = spread_shares(out, start, share, s1, r1)
    sums[...] = jnp.zeros_like(sums)
    for row, term in enumerate((values, total * unit, total, back_rows)):
        sums[row : row + 1] = jnp.sum(jnp.sum(term, axis=0), axis=0, keepdims=True)
    for copy in copies:
        copy.wait()


def share_scratch(parts, copies):
    ways = lax.axis_size("tensor")
    batch, tokens, model = parts.shape
    return [pltpu.VMEM((ways - 1, batch, tokens // ways, model), LOW)] + [
        pltpu.SemaphoreType.DMA((ways - 1,))
    ] * copies


def forward_share(parts, inputs, table):
    ways = lax.axis_size("tensor")
    batch, tokens, model = parts.shape
    return pl.pallas_call(
        forward_share_kernel,
        out_shape=(
            jax.ShapeDtypeStruct(parts.shape, LOW),
            jax.ShapeDtypeStruct((batch, tokens // ways, model), F32),
        ),
        in_specs=whole(3),
        out_specs=tuple(whole(2)),
        scratch_shapes=share_scratch(parts, 4),
        compiler_params=params(4),
    )(parts, inputs, table)


def backward_share(parts, back, middle, table):
    return pl.pallas_call(
        backward_share_kernel,
        out_shape=(
            jax.ShapeDtypeStruct(parts.shape, LOW),
            jax.ShapeDtypeStruct(middle.shape, F32),
            jax.ShapeDtypeStruct((8, parts.shape[2]), F32),
        ),
        in_specs=whole(4),
        out_specs=tuple(whole(3)),
        scratch_shapes=share_scratch(parts, 4),
        compiler_params=params(5),
    )(parts, back, middle, table)


def final_kernel(
    grads, first_part, down_part, inputs, middle, middle_grad, table, owned,
    grad_sum, input_grad, result, vector_sum,
    land_dp, pass_on, land_ctx, land_first, land_down, land_t, land_c, land_d,
    xs, xr, zs, zr, fs, fr, ds, dr, ts, tr, cs, cr, es, er,
):
    groups, rows = lax.axis_size("dp"), lax.axis_size("ctx")
    me_dp, me_ctx = lax.axis_index("dp"), lax.axis_index("ctx")
    share = middle.shape[1]
    start = pl.multiple_of(lax.axis_index("tensor") * share, share)
    greet(("dp", "ctx", "tensor"))
    order = list(range(1, rows)) + [0]
    across = {}
    for step in order:
        for far in range(1, groups):
            peer = place("dp", far)
            across[step, far] = push(
                grads.at[peer, place("ctx", step)],
                land_dp.at[step, far - 1],
                xs.at[step, far - 1],
                xr.at[step, far - 1],
                {"dp": peer},
            )
    first_copies = start_shares(first_part, land_first, fs, fr)
    down_copies = start_shares(down_part, land_down, ds, dr)

    along = []
    for step in order:
        owner = place("ctx", step)
        for far in range(1, groups):
            across[step, far].wait()
        total = grads[me_dp, owner].astype(F32)
        for far in range(1, groups):
            total = total + land_dp[step, far - 1].astype(F32)
        if step == 0:
            grad_sum[...] = total
        else:
            pass_on[step - 1] = total.astype(LOW)
            along.append(
                push(
                    pass_on.at[step - 1],
                    land_ctx.at[step - 1],
                    zs.at[step - 1],
                    zr.at[step - 1],
                    {"ctx": owner},
                )
            )

    for copy in first_copies:
        copy.wait()
    total = sum_shares(first_part, land_first, start)
    unit, scale = unit_norm(inputs[:, pl.ds(start, share), :].astype(F32))
    input_grad[...] = middle_grad[...] + norm_back(total, table[0:1][None], unit, scale)
    vector_sum[...] = owned[...]
    vector_sum[0:1] = jnp.sum(jnp.sum(total * unit, axis=0), axis=0, keepdims=True)
    vector_sum[1:2] = jnp.sum(jnp.sum(total, axis=0), axis=0, keepdims=True)
    for axis, land, sends, receives in (
        ("tensor", land_t, ts, tr),
        ("ctx", land_c, cs, cr),
        ("dp", land_d, es, er),
    ):
        copies = [
            push(
                vector_sum,
                land.at[step - 1],
                sends.at[step - 1],
                receives.at[step - 1],
                {axis: place(axis, step)},
            )
            for step in range(1, lax.axis_size(axis))
        ]
        for copy in copies:
            copy.wait()
        summed = vector_sum[...]
        for step in range(1, lax.axis_size(axis)):
            summed = summed + land[step - 1]
        vector_sum[...] = summed

    for copy in down_copies:
        copy.wait()
    total = sum_shares(down_part, land_down, start)
    result[...] = (middle[...] + total + table[7:8][None]).astype(LOW)
    for copy in along:
        copy.wait()
    summed = grad_sum[...]
    for step in range(1, rows):
        summed = summed + land_ctx[step - 1].astype(F32)
    grad_sum[...] = summed


def finish(grads, first_part, down_part, inputs, middle, middle_grad, table, owned):
    groups, rows = lax.axis_size("dp"), lax.axis_size("ctx")
    ways = lax.axis_size("tensor")
    block = grads.shape[2:]
    dma = pltpu.SemaphoreType.DMA
    land = pltpu.VMEM((ways - 1,) + middle.shape, LOW)
    pairs = ((rows, groups - 1), (rows - 1,), (ways - 1,), (ways - 1,))
    pairs += ((ways - 1,), (rows - 1,), (groups - 1,))
    return pl.pallas_call(
        final_kernel,
        out_shape=(
            jax.ShapeDtypeStruct(block, F32),
            jax.ShapeDtypeStruct(middle.shape, F32),
            jax.ShapeDtypeStruct(middle.shape, LOW),
            jax.ShapeDtypeStruct(owned.shape, F32),
        ),
        in_specs=whole(8),
        out_specs=tuple(whole(4)),
        scratch_shapes=[
            pltpu.VMEM((rows, groups - 1) + block, LOW),
            pltpu.VMEM((rows - 1,) + block, LOW),
            pltpu.VMEM((rows - 1,) + block, LOW),
            land,
            land,
            pltpu.VMEM((ways - 1,) + owned.shape, F32),
            pltpu.VMEM((rows - 1,) + owned.shape, F32),
            pltpu.VMEM((groups - 1,) + owned.shape, F32),
        ]
        + [dma(shape) for shape in pairs for _ in range(2)],
        compiler_params=params(6),
    )(grads, first_part, down_part, inputs, middle, middle_grad, table, owned)


def allowed_pairs(segment, tokens):
    ctx_index = lax.axis_index("ctx")
    key_places = jnp.arange(segment.shape[1], dtype=jnp.int32)
    query_places = ctx_index * tokens + jnp.arange(tokens, dtype=jnp.int32)
    query_segment = lax.dynamic_slice_in_dim(segment, ctx_index * tokens, tokens, 1)
    return (query_places[None, :, None] >= key_places[None, None, :]) & (
        query_segment[:, :, None] == segment[:, None, :]
    )


def heads_of(values):
    batch, tokens, width = values.shape
    return values.reshape(batch, tokens, width // HD, HD)


def attend(query, keys, values, allowed):
    scores = jnp.einsum(
        "bqhd,bkhd->bhqk", heads_of(query), heads_of(keys), preferred_element_type=F32
    ) * HD ** (-0.5)
    scores = jnp.where(allowed[:, None], scores, -1e30)
    weights = jnp.exp(scores - jnp.max(scores, axis=-1, keepdims=True))
    probs = weights / jnp.sum(weights, axis=-1, keepdims=True)
    mixed = jnp.einsum(
        "bhqk,bkhd->bqhd", probs.astype(LOW), heads_of(values), preferred_element_type=F32
    )
    return mixed.reshape(query.shape).astype(LOW), probs


def attend_back(mixed_grad, query, keys, values, probs):
    grad_heads = heads_of(mixed_grad)
    prob_grad = jnp.einsum(
        "bqhd,bkhd->bhqk", grad_heads, heads_of(values), preferred_element_type=F32
    )
    row_delta = jnp.sum(prob_grad * probs, axis=-1, keepdims=True)
    score_grad = (probs * (prob_grad - row_delta) * HD ** (-0.5)).astype(LOW)
    query_grad = jnp.einsum(
        "bhqk,bkhd->bqhd", score_grad, heads_of(keys), preferred_element_type=F32
    ).reshape(query.shape)
    key_grad = jnp.einsum(
        "bhqk,bqhd->bkhd", score_grad, heads_of(query), preferred_element_type=F32
    ).reshape(keys.shape)
    value_grad = jnp.einsum(
        "bhqk,bqhd->bkhd", probs.astype(LOW), grad_heads, preferred_element_type=F32
    ).reshape(keys.shape)
    return query_grad, key_grad, value_grad


def on_device(
    hidden_in,
    cotangent,
    segment_ids,
    qkv_weight,
    qkv_first,
    qkv_second,
    out_weight,
    out_first,
    out_second,
    up_weight,
    up_first,
    up_second,
    down_weight,
    down_first,
    down_second,
    vectors,
    vectors_first,
    vectors_second,
):
    batch, tokens, model = hidden_in.shape
    width = qkv_weight.shape[2]
    units = up_weight.shape[1]
    rows_all = batch * tokens
    tensor_index = lax.axis_index("tensor")

    shard = jnp.concatenate(
        [qkv_weight[0], qkv_weight[1], qkv_weight[2], out_weight.T, up_weight, down_weight.T],
        axis=1,
    ).astype(LOW)
    table_rows, part = vectors.shape
    pad_rows = -table_rows % 16
    small = jnp.pad(vectors.astype(LOW), ((0, pad_rows), (0, -part % 128)))
    gathered, small_all = gather_weights(shard, small)
    gathered = gathered.reshape(model, shard.shape[1])
    small_all = small_all.reshape((-1,) + small.shape)[:, :, :part]
    table = small_all.transpose(1, 0, 2).reshape(small.shape[0], model).astype(F32)
    proj = gathered[:, : 3 * width]
    out_turned = gathered[:, 3 * width : 4 * width]
    up = gathered[:, 4 * width : 4 * width + units]
    down_turned = gathered[:, 4 * width + units :]

    unit_first, _ = unit_norm(hidden_in.astype(F32))
    first_norm = (unit_first * table[0] + table[1]).astype(LOW).reshape(rows_all, model)
    projected = dot(first_norm, proj, 1, 0)
    query_bias = lax.dynamic_slice_in_dim(table[2], tensor_index * width, width)
    value_bias = lax.dynamic_slice_in_dim(table[3], tensor_index * width, width)
    query = (projected[:, :width] + query_bias).astype(LOW).reshape(batch, tokens, width)
    local_kv = (
        jnp.concatenate(
            [projected[:, width : 2 * width], projected[:, 2 * width :] + value_bias], axis=1
        )
        .astype(LOW)
        .reshape(batch, tokens, 2 * width)
    )
    all_kv = gather_ctx(local_kv)
    keys, values = all_kv[..., :width], all_kv[..., width:]
    allowed = allowed_pairs(segment_ids, tokens)
    mixed, probs = attend(query, keys, values, allowed)
    mixed = mixed.reshape(rows_all, width)

    attn_part = dot(mixed, out_turned, 1, 1).astype(LOW).reshape(batch, tokens, model)
    second_norm, middle = forward_share(attn_part, hidden_in, table)
    second_norm = second_norm.reshape(rows_all, model)
    unit_bias = lax.dynamic_slice_in_dim(
        table[8:table_rows].reshape(-1), tensor_index * units, units
    )
    hidden = dot(second_norm, up, 1, 0) + unit_bias
    gelu_value, gelu_pull = jax.vjp(jax.nn.gelu, hidden)
    active = gelu_value.astype(LOW)
    down_part = dot(active, down_turned, 1, 1).astype(LOW).reshape(batch, tokens, model)

    back = cotangent.reshape(rows_all, model)
    hidden_grad = gelu_pull(dot(back, down_turned, 1, 0))[0]
    hidden_low = hidden_grad.astype(LOW)
    second_part = dot(hidden_low, up, 1, 1).astype(LOW).reshape(batch, tokens, model)
    middle_low, middle_grad, late_rows = backward_share(second_part, cotangent, middle, table)
    grad_down = dot(back, active, 0, 0)
    grad_up = dot(second_norm, hidden_low, 0, 0)

    middle_low = middle_low.reshape(rows_all, model)
    mixed_grad = dot(middle_low, out_turned, 1, 0).astype(LOW).reshape(batch, tokens, width)
    query_grad, key_part, value_part = attend_back(mixed_grad, query, keys, values, probs)
    kv_grad = scatter_ctx(jnp.concatenate([key_part, value_part], axis=2).astype(LOW))
    grad_out = dot(middle_low, mixed, 0, 0)
    stacked = jnp.concatenate([query_grad.astype(LOW), kv_grad], axis=2).reshape(
        rows_all, 3 * width
    )
    first_part = dot(stacked, proj, 1, 1).astype(LOW).reshape(batch, tokens, model)
    grad_qkv = dot(first_norm, stacked, 0, 0)
    grads = jnp.concatenate([grad_qkv, grad_out, grad_up, grad_down], axis=1).astype(LOW)
    grads = grads.reshape((lax.axis_size("dp"), lax.axis_size("ctx")) + shard.shape)

    owned = jnp.zeros((small.shape[0] * model,), F32)
    owned = lax.dynamic_update_slice(
        owned, jnp.sum(query_grad, axis=(0, 1)), (2 * model + tensor_index * width,)
    )
    owned = lax.dynamic_update_slice(
        owned, jnp.sum(value_part, axis=(0, 1)), (3 * model + tensor_index * width,)
    )
    owned = lax.dynamic_update_slice(owned, late_rows[:4].reshape(-1), (4 * model,))
    owned = lax.dynamic_update_slice(
        owned, jnp.sum(hidden_grad, axis=0), (8 * model + tensor_index * units,)
    ).reshape(small.shape[0], model)

    grad_sum, input_grad, result, vector_sum = finish(
        grads, first_part, down_part, hidden_in, middle, middle_grad, table, owned
    )
    grad_vectors = lax.dynamic_slice_in_dim(
        vector_sum[:table_rows],
        (lax.axis_index("dp") * lax.axis_size("ctx") + lax.axis_index("ctx")) * part,
        part,
        1,
    )
    qkv_sum = jnp.stack([grad_sum[:, at * width : (at + 1) * width] for at in range(3)])
    out_sum = grad_sum[:, 3 * width : 4 * width].T
    up_sum = grad_sum[:, 4 * width : 4 * width + units]
    down_sum = grad_sum[:, 4 * width + units :].T
    return (
        result,
        input_grad,
        *adamw(qkv_weight, qkv_first, qkv_second, qkv_sum, rate_qkv, weight_decay),
        *adamw(out_weight, out_first, out_second, out_sum, rate_out, weight_decay),
        *adamw(up_weight, up_first, up_second, up_sum, rate_up, weight_decay),
        *adamw(down_weight, down_first, down_second, down_sum, rate_down, weight_decay),
        *adamw(vectors, vectors_first, vectors_second, grad_vectors, rate_vectors, 0.0),
    )


def solution(mesh):
    tokens = P("dp", "ctx", None)
    shares = P("dp", ("ctx", "tensor"), None)
    by_row = P(("dp", "ctx"), "tensor")
    by_column = P("tensor", ("dp", "ctx"))
    stacked = P(None, ("dp", "ctx"), "tensor")
    narrow = P(None, ("dp", "ctx"))
    states = (stacked,) * 3 + (by_column,) * 3 + (by_row,) * 3 + (by_column,) * 3 + (narrow,) * 3
    return jax.shard_map(
        on_device,
        mesh=mesh,
        in_specs=(tokens, tokens, P("dp", None)) + states,
        out_specs=(shares, shares) + states,
        check_vma=False,
    )
```

```python
import functools

import jax
import jax.numpy as jnp
from jax import lax
from jax.experimental import pallas as pl
from jax.experimental.pallas import tpu as pltpu
from jax.sharding import PartitionSpec as P

HD = 64
STEP = 10

norm_eps = 1e-05
beta_first = 0.9
beta_second = 0.999
adam_eps = 1e-08
weight_decay = 0.01
rate_qkv = 0.05
rate_out = 0.2
rate_up = 0.05
rate_down = 0.025
rate_vectors = 0.3

LOW = jnp.bfloat16
F32 = jnp.float32


def dot(left, right, left_dim, right_dim):
    return lax.dot_general(
        left, right, (((left_dim,), (right_dim,)), ((), ())), preferred_element_type=F32
    )


def unit_norm(values):
    centre = values - jnp.mean(values, axis=-1, keepdims=True)
    scale = lax.rsqrt(jnp.mean(centre * centre, axis=-1, keepdims=True) + norm_eps)
    return centre * scale, scale


def norm_back(grad, gain, unit, scale):
    inner = grad * gain
    return scale * (
        inner
        - jnp.mean(inner, axis=-1, keepdims=True)
        - unit * jnp.mean(inner * unit, axis=-1, keepdims=True)
    )


def adamw(weight, first, second, grad, rate, decay):
    first_new = beta_first * first + (1.0 - beta_first) * grad
    second_new = beta_second * second + (1.0 - beta_second) * grad * grad
    fix_first = 1.0 - beta_first**STEP
    fix_second = 1.0 - beta_second**STEP
    update = first_new / fix_first / (jnp.sqrt(second_new / fix_second) + adam_eps)
    return (weight - rate * (update + decay * weight), first_new, second_new)


def whole(count):
    return [pl.BlockSpec(memory_space=pltpu.VMEM)] * count


def params(number):
    return pltpu.CompilerParams(
        collective_id=number, has_side_effects=True, vmem_limit_bytes=48 * 2**20
    )


def place(axis, step):
    size = lax.axis_size(axis)
    return lax.rem(lax.axis_index(axis) + step + size, size)


def push(source, target, sends, receives, device):
    copy = pltpu.make_async_remote_copy(
        src_ref=source,
        dst_ref=target,
        send_sem=sends,
        recv_sem=receives,
        device_id=device,
        device_id_type=pl.DeviceIdType.MESH,
    )
    copy.start()
    return copy


def greet(axes):
    barrier = pltpu.get_barrier_semaphore()
    count = 0
    for axis in axes:
        for step in range(1, lax.axis_size(axis)):
            pl.semaphore_signal(
                barrier,
                inc=1,
                device_id={axis: place(axis, step)},
                device_id_type=pl.DeviceIdType.MESH,
            )
            count += 1
    pl.semaphore_wait(barrier, count)


def weights_kernel(shard, small, out, small_out, zs, zr, xs, xr, szs, szr, sxs, sxr):
    groups, rows = lax.axis_size("dp"), lax.axis_size("ctx")
    me_dp, me_ctx = lax.axis_index("dp"), lax.axis_index("ctx")
    greet(("dp", "ctx"))
    waits = []
    along = []
    for source, target, sends, receives in ((small, small_out, szs, szr), (shard, out, zs, zr)):
        for step in range(1, rows):
            along.append(
                push(
                    source,
                    target.at[me_dp, me_ctx],
                    sends.at[step - 1],
                    receives.at[step - 1],
                    {"ctx": place("ctx", step)},
                )
            )
    across = []
    arrived = iter(along)
    for source, target, sends, receives in ((small, small_out, sxs, sxr), (shard, out, xs, xr)):
        target[me_dp, me_ctx] = source[...]
        for step in range(rows):
            owner = place("ctx", -step)
            if step > 0:
                next(arrived).wait_recv()
            block = source if step == 0 else target.at[me_dp, owner]
            for far in range(1, groups):
                across.append(
                    push(
                        block,
                        target.at[me_dp, owner],
                        sends.at[step, far - 1],
                        receives.at[step, far - 1],
                        {"dp": place("dp", far)},
                    )
                )
    for copy in across:
        copy.wait_recv()
    for copy in along + across:
        copy.wait_send()


def gather_weights(shard, small):
    groups, rows = lax.axis_size("dp"), lax.axis_size("ctx")
    dma = pltpu.SemaphoreType.DMA
    one = [dma((max(rows - 1, 1),))] * 2 + [dma((rows, max(groups - 1, 1)))] * 2
    return pl.pallas_call(
        weights_kernel,
        out_shape=(
            jax.ShapeDtypeStruct((groups, rows) + shard.shape, shard.dtype),
            jax.ShapeDtypeStruct((groups, rows) + small.shape, small.dtype),
        ),
        in_specs=whole(2),
        out_specs=tuple(whole(2)),
        scratch_shapes=one + one,
        compiler_params=params(1),
    )(shard, small)


def head_lanes(width, offset, head):
    lanes = lax.broadcasted_iota(jnp.int32, (1, width), 1) - offset
    return ((lanes >= head * HD) & (lanes < (head + 1) * HD)).astype(F32)


def softmax_of(query, keys, allowed):
    scores = dot(query, keys, 1, 1) * HD ** (-0.5)
    scores = jnp.where(allowed, scores, -1e30)
    weights = jnp.exp(scores - jnp.max(scores, axis=-1, keepdims=True))
    return weights * (1.0 / jnp.sum(weights, axis=-1, keepdims=True))


def allowed_pairs(segment_row, segment_column):
    tokens, length = segment_column.shape[0], segment_row.shape[1]
    first = lax.axis_index("ctx") * tokens
    queries = first + lax.broadcasted_iota(jnp.int32, (tokens, length), 0)
    keys = lax.broadcasted_iota(jnp.int32, (tokens, length), 1)
    return (queries >= keys) & (segment_column == segment_row)


def attend_kernel(
    width, local, query, segment_row, segment_column, shard,
    all_kv, mixed, out,
    total, ks, kr, zs, zr, xs, xr,
):
    groups, rows = lax.axis_size("dp"), lax.axis_size("ctx")
    me_dp, me_ctx = lax.axis_index("dp"), lax.axis_index("ctx")
    batch, tokens = local.shape[:2]
    key_width, value_width = query.shape[2], mixed.shape[2]
    lead = 2 * width - value_width
    start = pl.multiple_of(me_ctx * tokens, tokens)
    greet(("dp", "ctx"))
    kv_copies = [
        push(
            local,
            all_kv.at[:, pl.ds(start, tokens), :],
            ks.at[step - 1],
            kr.at[step - 1],
            {"ctx": place("ctx", step)},
        )
        for step in range(1, rows)
    ]
    along = [
        push(
            shard,
            out.at[me_dp, me_ctx],
            zs.at[step - 1],
            zr.at[step - 1],
            {"ctx": place("ctx", step)},
        )
        for step in range(1, rows)
    ]
    across = []

    def send_across(step):
        owner = place("ctx", -step)
        block = shard if step == 0 else out.at[me_dp, owner]
        for far in range(1, groups):
            across.append(
                push(
                    block,
                    out.at[me_dp, owner],
                    xs.at[step, far - 1],
                    xr.at[step, far - 1],
                    {"dp": place("dp", far)},
                )
            )

    send_across(0)
    all_kv[:, pl.ds(start, tokens), :] = local[...]
    out[me_dp, me_ctx] = shard[...]
    for copy in kv_copies:
        copy.wait()
    for one in range(batch):
        allowed = allowed_pairs(segment_row[one], segment_column[one])
        total[...] = jnp.zeros_like(total)

        def one_head(head, carry):
            masked = query[one] * head_lanes(key_width, 0, head).astype(LOW)
            probs = softmax_of(masked, all_kv[one, :, :key_width], allowed)
            part = dot(probs.astype(LOW), all_kv[one, :, lead:], 1, 0)
            total[...] += part * head_lanes(value_width, width - lead, head)
            return carry

        lax.fori_loop(0, width // HD, one_head, 0)
        mixed[one] = total[...].astype(LOW)
        if one == 0:
            for step in range(1, rows):
                along[step - 1].wait_recv()
                send_across(step)
    for copy in across:
        copy.wait_recv()
    for copy in along + across:
        copy.wait_send()


def attend(width, local, query, segment_row, segment_column, shard):
    groups, rows = lax.axis_size("dp"), lax.axis_size("ctx")
    batch, tokens = local.shape[:2]
    value_width = 2 * width - width // 128 * 128
    dma = pltpu.SemaphoreType.DMA
    return pl.pallas_call(
        functools.partial(attend_kernel, width),
        out_shape=(
            jax.ShapeDtypeStruct((batch, rows * tokens, 2 * width), LOW),
            jax.ShapeDtypeStruct((batch, tokens, value_width), LOW),
            jax.ShapeDtypeStruct((groups, rows) + shard.shape, LOW),
        ),
        in_specs=whole(5),
        out_specs=tuple(whole(3)),
        scratch_shapes=[pltpu.VMEM((tokens, value_width), F32)]
        + [dma((rows - 1,))] * 4
        + [dma((rows, groups - 1))] * 2,
        compiler_params=params(2),
    )(local, query, segment_row, segment_column, shard)


def attend_back_kernel(
    width, mixed_grad, query, all_kv, segment_row, segment_column, g0, g1, g2,
    kv_grad, query_grad, value_sum, sum0, sum1, sum2,
    total, parts, landing, dp0, dp1, dp2, pass0, pass1, pass2, ctx0, ctx1, ctx2,
    ks, kr, xs, xr, zs, zr,
):
    groups, rows = lax.axis_size("dp"), lax.axis_size("ctx")
    me_dp, me_ctx = lax.axis_index("dp"), lax.axis_index("ctx")
    batch, tokens = kv_grad.shape[:2]
    key_width, value_width = query.shape[2], mixed_grad.shape[2]
    lead = 2 * width - value_width
    weights = (
        (g0, sum0, dp0, pass0, ctx0),
        (g1, sum1, dp1, pass1, ctx1),
        (g2, sum2, dp2, pass2, ctx2),
    )
    order = list(range(1, rows)) + [0]
    greet(("dp", "ctx"))
    across, along = {}, []
    for step in order:
        for at, (grads, _, land_dp, _, _) in enumerate(weights):
            for far in range(1, groups):
                peer = place("dp", far)
                across[step, at, far] = push(
                    grads.at[peer, place("ctx", step)],
                    land_dp.at[step, far - 1],
                    xs.at[at, step, far - 1],
                    xr.at[at, step, far - 1],
                    {"dp": peer},
                )
    value_sum[...] = jnp.zeros_like(value_sum)
    kv_copies = []
    for one in range(batch):
        allowed = allowed_pairs(segment_row[one], segment_column[one])
        total[...] = jnp.zeros_like(total)
        query_grad[one] = jnp.zeros(query_grad.shape[1:], F32)

        def one_head(head, carry):
            lanes = head_lanes(key_width, 0, head)
            masked = query[one] * lanes.astype(LOW)
            keys = all_kv[one, :, :key_width]
            probs = softmax_of(masked, keys, allowed)
            masked_grad = mixed_grad[one] * head_lanes(value_width, width - lead, head).astype(LOW)
            prob_grad = dot(masked_grad, all_kv[one, :, lead:], 1, 1)
            delta = jnp.sum(prob_grad * probs, axis=-1, keepdims=True)
            score_grad = (probs * (prob_grad - delta) * HD ** (-0.5)).astype(LOW)
            query_grad[one] += dot(score_grad, keys, 1, 0) * lanes
            total[:, :key_width] += dot(score_grad, masked, 0, 0)
            total[:, lead:] += dot(probs.astype(LOW), masked_grad, 0, 0)
            return carry

        lax.fori_loop(0, width // HD, one_head, 0)
        value_sum[0:1] += jnp.sum(total[...], axis=0, keepdims=True)
        parts[one] = total[...].astype(LOW)
        for step in range(1, rows):
            peer = place("ctx", step)
            kv_copies.append(
                push(
                    parts.at[one, pl.ds(pl.multiple_of(peer * tokens, tokens), tokens), :],
                    landing.at[step - 1, one],
                    ks.at[one, step - 1],
                    kr.at[one, step - 1],
                    {"ctx": peer},
                )
            )
        if one == 0:
            for step in order:
                owner = place("ctx", step)
                for at, (grads, summed, land_dp, pass_on, land_ctx) in enumerate(weights):
                    for far in range(1, groups):
                        across[step, at, far].wait()
                    value = grads[me_dp, owner].astype(F32)
                    for far in range(1, groups):
                        value = value + land_dp[step, far - 1].astype(F32)
                    if step == 0:
                        summed[...] = value
                    else:
                        pass_on[step - 1] = value.astype(LOW)
                        along.append(
                            push(
                                pass_on.at[step - 1],
                                land_ctx.at[step - 1],
                                zs.at[at, step - 1],
                                zr.at[at, step - 1],
                                {"ctx": owner},
                            )
                        )
    start = pl.multiple_of(me_ctx * tokens, tokens)
    for copy in kv_copies:
        copy.wait()
    value = parts[:, pl.ds(start, tokens), :].astype(F32)
    for step in range(1, rows):
        value = value + landing[step - 1].astype(F32)
    kv_grad[...] = value.astype(LOW)
    for copy in along:
        copy.wait()
    for _, summed, _, _, land_ctx in weights:
        value = summed[...]
        for step in range(1, rows):
            value = value + land_ctx[step - 1].astype(F32)
        summed[...] = value


def attend_back(width, mixed_grad, query, all_kv, segment_row, segment_column, weight_grads):
    groups, rows = lax.axis_size("dp"), lax.axis_size("ctx")
    batch, tokens, key_width = query.shape
    length = rows * tokens
    blocks = [grads.shape[2:] for grads in weight_grads]
    dma = pltpu.SemaphoreType.DMA
    return pl.pallas_call(
        functools.partial(attend_back_kernel, width),
        out_shape=(
            jax.ShapeDtypeStruct((batch, tokens, 2 * width), LOW),
            jax.ShapeDtypeStruct(query.shape, F32),
            jax.ShapeDtypeStruct((8, 2 * width), F32),
        )
        + tuple(jax.ShapeDtypeStruct(block, F32) for block in blocks),
        in_specs=whole(8),
        out_specs=tuple(whole(6)),
        scratch_shapes=[
            pltpu.VMEM((length, 2 * width), F32),
            pltpu.VMEM((batch, length, 2 * width), LOW),
            pltpu.VMEM((rows - 1, batch, tokens, 2 * width), LOW),
        ]
        + [pltpu.VMEM((rows, groups - 1) + block, LOW) for block in blocks]
        + [pltpu.VMEM((rows - 1,) + block, LOW) for block in blocks] * 2
        + [dma((batch, rows - 1))] * 2
        + [dma((3, rows, groups - 1))] * 2
        + [dma((3, rows - 1))] * 2,
        compiler_params=params(3),
    )(mixed_grad, query, all_kv, segment_row, segment_column, *weight_grads)


def start_shares(parts, landing, sends, receives):
    share = landing.shape[2]
    copies = []
    for step in range(1, lax.axis_size("tensor")):
        peer = place("tensor", step)
        copies.append(
            push(
                parts.at[:, pl.ds(pl.multiple_of(peer * share, share), share), :],
                landing.at[step - 1],
                sends.at[step - 1],
                receives.at[step - 1],
                {"tensor": peer},
            )
        )
    return copies


def sum_shares(parts, landing, start):
    total = parts[:, pl.ds(start, landing.shape[2]), :].astype(F32)
    for step in range(landing.shape[0]):
        total = total + landing[step].astype(F32)
    return total


def spread_shares(out, start, share, sends, receives):
    copies = []
    for step in range(1, lax.axis_size("tensor")):
        mine = out.at[:, pl.ds(start, share), :]
        copies.append(
            push(
                mine, mine, sends.at[step - 1], receives.at[step - 1], {"tensor": place("tensor", step)}
            )
        )
    return copies


def forward_share_kernel(parts, inputs, table, out, middle, landing, s0, r0, s1, r1):
    share = middle.shape[1]
    start = pl.multiple_of(lax.axis_index("tensor") * share, share)
    greet(("tensor",))
    copies = start_shares(parts, landing, s0, r0)
    for copy in copies:
        copy.wait()
    total = sum_shares(parts, landing, start)
    values = inputs[:, pl.ds(start, share), :].astype(F32) + total + table[4:5][None]
    middle[...] = values
    unit, scale = unit_norm(values)
    out[:, pl.ds(start, share), :] = (unit * table[5:6][None] + table[6:7][None]).astype(LOW)
    for copy in spread_shares(out, start, share, s1, r1):
        copy.wait()


def backward_share_kernel(parts, back, middle, table, out, grad, sums, landing, s0, r0, s1, r1):
    share = middle.shape[1]
    start = pl.multiple_of(lax.axis_index("tensor") * share, share)
    greet(("tensor",))
    copies = start_shares(parts, landing, s0, r0)
    back_rows = back[:, pl.ds(start, share), :].astype(F32)
    unit, scale = unit_norm(middle[...])
    for copy in copies:
        copy.wait()
    total = sum_shares(parts, landing, start)
    values = back_rows + norm_back(total, table[5:6][None], unit, scale)
    grad[...] = values
    out[:, pl.ds(start, share), :] = values.astype(LOW)
    copies = spread_shares(out, start, share, s1, r1)
    sums[...] = jnp.zeros_like(sums)
    for row, term in enumerate((values, total * unit, total, back_rows)):
        sums[row : row + 1] = jnp.sum(jnp.sum(term, axis=0), axis=0, keepdims=True)
    for copy in copies:
        copy.wait()


def share_scratch(parts, copies):
    ways = lax.axis_size("tensor")
    batch, tokens, model = parts.shape
    return [pltpu.VMEM((ways - 1, batch, tokens // ways, model), LOW)] + [
        pltpu.SemaphoreType.DMA((ways - 1,))
    ] * copies


def forward_share(parts, inputs, table):
    ways = lax.axis_size("tensor")
    batch, tokens, model = parts.shape
    return pl.pallas_call(
        forward_share_kernel,
        out_shape=(
            jax.ShapeDtypeStruct(parts.shape, LOW),
            jax.ShapeDtypeStruct((batch, tokens // ways, model), F32),
        ),
        in_specs=whole(3),
        out_specs=tuple(whole(2)),
        scratch_shapes=share_scratch(parts, 4),
        compiler_params=params(4),
    )(parts, inputs, table)


def backward_share(parts, back, middle, table):
    return pl.pallas_call(
        backward_share_kernel,
        out_shape=(
            jax.ShapeDtypeStruct(parts.shape, LOW),
            jax.ShapeDtypeStruct(middle.shape, F32),
            jax.ShapeDtypeStruct((8, parts.shape[2]), F32),
        ),
        in_specs=whole(4),
        out_specs=tuple(whole(3)),
        scratch_shapes=share_scratch(parts, 4),
        compiler_params=params(5),
    )(parts, back, middle, table)


def final_kernel(
    grads, first_part, down_part, inputs, middle, middle_grad, table, owned,
    grad_sum, input_grad, result, vector_sum,
    land_dp, pass_on, land_ctx, land_first, land_down, land_t, land_c, land_d,
    xs, xr, zs, zr, fs, fr, ds, dr, ts, tr, cs, cr, es, er,
):
    groups, rows = lax.axis_size("dp"), lax.axis_size("ctx")
    me_dp, me_ctx = lax.axis_index("dp"), lax.axis_index("ctx")
    share = middle.shape[1]
    start = pl.multiple_of(lax.axis_index("tensor") * share, share)
    greet(("dp", "ctx", "tensor"))
    order = list(range(1, rows)) + [0]
    across = {}
    for step in order:
        for far in range(1, groups):
            peer = place("dp", far)
            across[step, far] = push(
                grads.at[peer, place("ctx", step)],
                land_dp.at[step, far - 1],
                xs.at[step, far - 1],
                xr.at[step, far - 1],
                {"dp": peer},
            )
    first_copies = start_shares(first_part, land_first, fs, fr)
    down_copies = start_shares(down_part, land_down, ds, dr)

    along = []
    for step in order:
        owner = place("ctx", step)
        for far in range(1, groups):
            across[step, far].wait()
        total = grads[me_dp, owner].astype(F32)
        for far in range(1, groups):
            total = total + land_dp[step, far - 1].astype(F32)
        if step == 0:
            grad_sum[...] = total
        else:
            pass_on[step - 1] = total.astype(LOW)
            along.append(
                push(
                    pass_on.at[step - 1],
                    land_ctx.at[step - 1],
                    zs.at[step - 1],
                    zr.at[step - 1],
                    {"ctx": owner},
                )
            )

    for copy in first_copies:
        copy.wait()
    total = sum_shares(first_part, land_first, start)
    unit, scale = unit_norm(inputs[:, pl.ds(start, share), :].astype(F32))
    input_grad[...] = middle_grad[...] + norm_back(total, table[0:1][None], unit, scale)
    vector_sum[...] = owned[...]
    vector_sum[0:1] = jnp.sum(jnp.sum(total * unit, axis=0), axis=0, keepdims=True)
    vector_sum[1:2] = jnp.sum(jnp.sum(total, axis=0), axis=0, keepdims=True)
    for axis, land, sends, receives in (
        ("tensor", land_t, ts, tr),
        ("ctx", land_c, cs, cr),
        ("dp", land_d, es, er),
    ):
        copies = [
            push(
                vector_sum,
                land.at[step - 1],
                sends.at[step - 1],
                receives.at[step - 1],
                {axis: place(axis, step)},
            )
            for step in range(1, lax.axis_size(axis))
        ]
        for copy in copies:
            copy.wait()
        summed = vector_sum[...]
        for step in range(1, lax.axis_size(axis)):
            summed = summed + land[step - 1]
        vector_sum[...] = summed

    for copy in down_copies:
        copy.wait()
    total = sum_shares(down_part, land_down, start)
    result[...] = (middle[...] + total + table[7:8][None]).astype(LOW)
    for copy in along:
        copy.wait()
    summed = grad_sum[...]
    for step in range(1, rows):
        summed = summed + land_ctx[step - 1].astype(F32)
    grad_sum[...] = summed


def finish(grads, first_part, down_part, inputs, middle, middle_grad, table, owned):
    groups, rows = lax.axis_size("dp"), lax.axis_size("ctx")
    ways = lax.axis_size("tensor")
    block = grads.shape[2:]
    dma = pltpu.SemaphoreType.DMA
    land = pltpu.VMEM((ways - 1,) + middle.shape, LOW)
    pairs = ((rows, groups - 1), (rows - 1,), (ways - 1,), (ways - 1,))
    pairs += ((ways - 1,), (rows - 1,), (groups - 1,))
    return pl.pallas_call(
        final_kernel,
        out_shape=(
            jax.ShapeDtypeStruct(block, F32),
            jax.ShapeDtypeStruct(middle.shape, F32),
            jax.ShapeDtypeStruct(middle.shape, LOW),
            jax.ShapeDtypeStruct(owned.shape, F32),
        ),
        in_specs=whole(8),
        out_specs=tuple(whole(4)),
        scratch_shapes=[
            pltpu.VMEM((rows, groups - 1) + block, LOW),
            pltpu.VMEM((rows - 1,) + block, LOW),
            pltpu.VMEM((rows - 1,) + block, LOW),
            land,
            land,
            pltpu.VMEM((ways - 1,) + owned.shape, F32),
            pltpu.VMEM((rows - 1,) + owned.shape, F32),
            pltpu.VMEM((groups - 1,) + owned.shape, F32),
        ]
        + [dma(shape) for shape in pairs for _ in range(2)],
        compiler_params=params(6),
    )(grads, first_part, down_part, inputs, middle, middle_grad, table, owned)


def on_device(
    hidden_in,
    cotangent,
    segment_ids,
    qkv_weight,
    qkv_first,
    qkv_second,
    out_weight,
    out_first,
    out_second,
    up_weight,
    up_first,
    up_second,
    down_weight,
    down_first,
    down_second,
    vectors,
    vectors_first,
    vectors_second,
):
    batch, tokens, model = hidden_in.shape
    width = qkv_weight.shape[2]
    units = up_weight.shape[1]
    rows_all = batch * tokens
    tensor_index = lax.axis_index("tensor")

    shard = jnp.concatenate([qkv_weight[0], qkv_weight[1], qkv_weight[2]], axis=1).astype(LOW)
    rest_shard = jnp.concatenate([up_weight, down_weight.T, out_weight.T], axis=1).astype(LOW)
    table_rows, part = vectors.shape
    pad_rows = -table_rows % 16
    small = jnp.pad(vectors.astype(LOW), ((0, pad_rows), (0, -part % 128)))
    gathered, small_all = gather_weights(shard, small)
    proj = gathered.reshape(model, shard.shape[1])
    small_all = small_all.reshape((-1,) + small.shape)[:, :, :part]
    table = small_all.transpose(1, 0, 2).reshape(small.shape[0], model).astype(F32)

    unit_first, _ = unit_norm(hidden_in.astype(F32))
    first_norm = (unit_first * table[0] + table[1]).astype(LOW).reshape(rows_all, model)
    projected = dot(first_norm, proj, 1, 0)
    query_bias = lax.dynamic_slice_in_dim(table[2], tensor_index * width, width)
    value_bias = lax.dynamic_slice_in_dim(table[3], tensor_index * width, width)
    query = (projected[:, :width] + query_bias).astype(LOW).reshape(batch, tokens, width)
    local_kv = (
        jnp.concatenate(
            [projected[:, width : 2 * width], projected[:, 2 * width :] + value_bias], axis=1
        )
        .astype(LOW)
        .reshape(batch, tokens, 2 * width)
    )
    lead = width // 128 * 128
    query = jnp.pad(query, ((0, 0), (0, 0), (0, -width % 128)))
    segment_row = segment_ids[:, None, :]
    segment_column = lax.dynamic_slice_in_dim(
        segment_ids, lax.axis_index("ctx") * tokens, tokens, 1
    )[:, :, None]
    all_kv, mixed, rest = attend(width, local_kv, query, segment_row, segment_column, rest_shard)
    rest = rest.reshape(model, rest_shard.shape[1])
    up = rest[:, :units]
    down_turned = rest[:, units : 2 * units]
    out_turned = rest[:, 2 * units :]
    mixed = mixed[:, :, width - lead :].reshape(rows_all, width)

    attn_part = dot(mixed, out_turned, 1, 1).astype(LOW).reshape(batch, tokens, model)
    second_norm, middle = forward_share(attn_part, hidden_in, table)
    second_norm = second_norm.reshape(rows_all, model)
    unit_bias = lax.dynamic_slice_in_dim(
        table[8:table_rows].reshape(-1), tensor_index * units, units
    )
    hidden = dot(second_norm, up, 1, 0) + unit_bias
    gelu_value, gelu_pull = jax.vjp(jax.nn.gelu, hidden)
    active = gelu_value.astype(LOW)
    down_part = dot(active, down_turned, 1, 1).astype(LOW).reshape(batch, tokens, model)

    back = cotangent.reshape(rows_all, model)
    hidden_grad = gelu_pull(dot(back, down_turned, 1, 0))[0]
    hidden_low = hidden_grad.astype(LOW)
    second_part = dot(hidden_low, up, 1, 1).astype(LOW).reshape(batch, tokens, model)
    middle_low, middle_grad, late_rows = backward_share(second_part, cotangent, middle, table)
    grad_down = dot(back, active, 0, 0)
    grad_up = dot(second_norm, hidden_low, 0, 0)

    middle_low = middle_low.reshape(rows_all, model)
    mixed_grad = dot(middle_low, out_turned, 1, 0).astype(LOW).reshape(batch, tokens, width)
    mixed_grad = jnp.pad(mixed_grad, ((0, 0), (0, 0), (width - lead, 0)))
    grad_out = dot(middle_low, mixed, 0, 0)
    blocks = (lax.axis_size("dp"), lax.axis_size("ctx"), shard.shape[0])
    weight_grads = [
        grads.astype(LOW).reshape(blocks + (-1,)) for grads in (grad_up, grad_down, grad_out)
    ]
    kv_grad, query_grad, value_sum, up_sum, down_sum, out_sum = attend_back(
        width, mixed_grad, query, all_kv, segment_row, segment_column, weight_grads
    )
    query_grad = query_grad[:, :, :width]
    stacked = jnp.concatenate([query_grad.astype(LOW), kv_grad], axis=2).reshape(
        rows_all, 3 * width
    )
    first_part = dot(stacked, proj, 1, 1).astype(LOW).reshape(batch, tokens, model)
    grad_qkv = dot(first_norm, stacked, 0, 0)
    grads = grad_qkv.astype(LOW).reshape(blocks + (-1,))

    owned = jnp.zeros((small.shape[0] * model,), F32)
    owned = lax.dynamic_update_slice(
        owned, jnp.sum(query_grad, axis=(0, 1)), (2 * model + tensor_index * width,)
    )
    owned = lax.dynamic_update_slice(
        owned, value_sum[0, width:], (3 * model + tensor_index * width,)
    )
    owned = lax.dynamic_update_slice(owned, late_rows[:4].reshape(-1), (4 * model,))
    owned = lax.dynamic_update_slice(
        owned, jnp.sum(hidden_grad, axis=0), (8 * model + tensor_index * units,)
    ).reshape(small.shape[0], model)

    grad_sum, input_grad, result, vector_sum = finish(
        grads, first_part, down_part, hidden_in, middle, middle_grad, table, owned
    )
    grad_vectors = lax.dynamic_slice_in_dim(
        vector_sum[:table_rows],
        (lax.axis_index("dp") * lax.axis_size("ctx") + lax.axis_index("ctx")) * part,
        part,
        1,
    )
    qkv_sum = jnp.stack([grad_sum[:, at * width : (at + 1) * width] for at in range(3)])
    out_sum = out_sum.T
    down_sum = down_sum.T
    return (
        result,
        input_grad,
        *adamw(qkv_weight, qkv_first, qkv_second, qkv_sum, rate_qkv, weight_decay),
        *adamw(out_weight, out_first, out_second, out_sum, rate_out, weight_decay),
        *adamw(up_weight, up_first, up_second, up_sum, rate_up, weight_decay),
        *adamw(down_weight, down_first, down_second, down_sum, rate_down, weight_decay),
        *adamw(vectors, vectors_first, vectors_second, grad_vectors, rate_vectors, 0.0),
    )


def solution(mesh):
    tokens = P("dp", "ctx", None)
    shares = P("dp", ("ctx", "tensor"), None)
    by_row = P(("dp", "ctx"), "tensor")
    by_column = P("tensor", ("dp", "ctx"))
    stacked = P(None, ("dp", "ctx"), "tensor")
    narrow = P(None, ("dp", "ctx"))
    states = (stacked,) * 3 + (by_column,) * 3 + (by_row,) * 3 + (by_column,) * 3 + (narrow,) * 3
    return jax.shard_map(
        on_device,
        mesh=mesh,
        in_specs=(tokens, tokens, P("dp", None)) + states,
        out_specs=(shares, shares) + states,
        check_vma=False,
    )
```

```python
import functools

import jax
import jax.numpy as jnp
from jax import lax
from jax.experimental import pallas as pl
from jax.experimental.pallas import tpu as pltpu
from jax.sharding import PartitionSpec as P

HD = 64
STEP = 10

norm_eps = 1e-05
beta_first = 0.9
beta_second = 0.999
adam_eps = 1e-08
weight_decay = 0.01
rate_qkv = 0.05
rate_out = 0.2
rate_up = 0.05
rate_down = 0.025
rate_vectors = 0.3

LOW = jnp.bfloat16
F32 = jnp.float32


def dot(left, right, left_dim, right_dim):
    return lax.dot_general(
        left, right, (((left_dim,), (right_dim,)), ((), ())), preferred_element_type=F32
    )


def unit_norm(values):
    centre = values - jnp.mean(values, axis=-1, keepdims=True)
    scale = lax.rsqrt(jnp.mean(centre * centre, axis=-1, keepdims=True) + norm_eps)
    return centre * scale, scale


def norm_back(grad, gain, unit, scale):
    inner = grad * gain
    return scale * (
        inner
        - jnp.mean(inner, axis=-1, keepdims=True)
        - unit * jnp.mean(inner * unit, axis=-1, keepdims=True)
    )


def adamw(weight, first, second, grad, rate, decay):
    first_new = beta_first * first + (1.0 - beta_first) * grad
    second_new = beta_second * second + (1.0 - beta_second) * grad * grad
    fix_first = 1.0 - beta_first**STEP
    fix_second = 1.0 - beta_second**STEP
    update = first_new / fix_first / (jnp.sqrt(second_new / fix_second) + adam_eps)
    return (weight - rate * (update + decay * weight), first_new, second_new)


def whole(count):
    return [pl.BlockSpec(memory_space=pltpu.VMEM)] * count


def params(number):
    return pltpu.CompilerParams(
        collective_id=number, has_side_effects=True, vmem_limit_bytes=48 * 2**20
    )


def place(axis, step):
    size = lax.axis_size(axis)
    return lax.rem(lax.axis_index(axis) + step + size, size)


def push(source, target, sends, receives, device):
    copy = pltpu.make_async_remote_copy(
        src_ref=source,
        dst_ref=target,
        send_sem=sends,
        recv_sem=receives,
        device_id=device,
        device_id_type=pl.DeviceIdType.MESH,
    )
    copy.start()
    return copy


def greet(axes):
    barrier = pltpu.get_barrier_semaphore()
    count = 0
    for axis in axes:
        for step in range(1, lax.axis_size(axis)):
            pl.semaphore_signal(
                barrier,
                inc=1,
                device_id={axis: place(axis, step)},
                device_id_type=pl.DeviceIdType.MESH,
            )
            count += 1
    pl.semaphore_wait(barrier, count)


def weights_kernel(shard, small, out, small_out, zs, zr, xs, xr, szs, szr, sxs, sxr):
    groups, rows = lax.axis_size("dp"), lax.axis_size("ctx")
    me_dp, me_ctx = lax.axis_index("dp"), lax.axis_index("ctx")
    greet(("dp", "ctx"))
    waits = []
    along = []
    for source, target, sends, receives in ((small, small_out, szs, szr), (shard, out, zs, zr)):
        for step in range(1, rows):
            along.append(
                push(
                    source,
                    target.at[me_dp, me_ctx],
                    sends.at[step - 1],
                    receives.at[step - 1],
                    {"ctx": place("ctx", step)},
                )
            )
    across = []
    arrived = iter(along)
    for source, target, sends, receives in ((small, small_out, sxs, sxr), (shard, out, xs, xr)):
        target[me_dp, me_ctx] = source[...]
        for step in range(rows):
            owner = place("ctx", -step)
            if step > 0:
                next(arrived).wait_recv()
            block = source if step == 0 else target.at[me_dp, owner]
            for far in range(1, groups):
                across.append(
                    push(
                        block,
                        target.at[me_dp, owner],
                        sends.at[step, far - 1],
                        receives.at[step, far - 1],
                        {"dp": place("dp", far)},
                    )
                )
    for copy in across:
        copy.wait_recv()
    for copy in along + across:
        copy.wait_send()


def gather_weights(shard, small):
    groups, rows = lax.axis_size("dp"), lax.axis_size("ctx")
    dma = pltpu.SemaphoreType.DMA
    one = [dma((max(rows - 1, 1),))] * 2 + [dma((rows, max(groups - 1, 1)))] * 2
    return pl.pallas_call(
        weights_kernel,
        out_shape=(
            jax.ShapeDtypeStruct((groups, rows) + shard.shape, shard.dtype),
            jax.ShapeDtypeStruct((groups, rows) + small.shape, small.dtype),
        ),
        in_specs=whole(2),
        out_specs=tuple(whole(2)),
        scratch_shapes=one + one,
        compiler_params=params(1),
    )(shard, small)


def head_lanes(width, offset, head):
    lanes = lax.broadcasted_iota(jnp.int32, (1, width), 1) - offset
    return ((lanes >= head * HD) & (lanes < (head + 1) * HD)).astype(F32)


def softmax_of(query, keys, allowed):
    scores = dot(query, keys, 1, 1) * HD ** (-0.5)
    scores = jnp.where(allowed, scores, -1e30)
    weights = jnp.exp(scores - jnp.max(scores, axis=-1, keepdims=True))
    return weights * (1.0 / jnp.sum(weights, axis=-1, keepdims=True))


def allowed_pairs(segment_row, segment_column):
    tokens, length = segment_column.shape[0], segment_row.shape[1]
    first = lax.axis_index("ctx") * tokens
    queries = first + lax.broadcasted_iota(jnp.int32, (tokens, length), 0)
    keys = lax.broadcasted_iota(jnp.int32, (tokens, length), 1)
    return (queries >= keys) & (segment_column == segment_row)


def attend_kernel(
    width, local, query, segment_row, segment_column, shard,
    all_kv, mixed, out,
    total, ks, kr, zs, zr, ys, yr, xs, xr,
):
    groups, rows = lax.axis_size("dp"), lax.axis_size("ctx")
    me_dp, me_ctx = lax.axis_index("dp"), lax.axis_index("ctx")
    batch, tokens = local.shape[:2]
    key_width, value_width = query.shape[2], mixed.shape[2]
    lead = 2 * width - value_width
    start = pl.multiple_of(me_ctx * tokens, tokens)
    greet(("dp", "ctx"))
    def hop(source, target, step, sign, sends, receives):
        owner = me_ctx - sign * step
        far = me_ctx + sign
        came = me_ctx - sign * (step + 1)
        copy = pltpu.make_async_remote_copy(
            src_ref=source if step == 0 else target(owner),
            dst_ref=target(owner),
            send_sem=sends.at[step],
            recv_sem=receives.at[step],
            device_id={"ctx": far},
            device_id_type=pl.DeviceIdType.MESH,
        )
        sent = (owner >= 0) & (owner < rows) & (far >= 0) & (far < rows)
        return copy, sent, (came >= 0) & (came < rows), came

    def kv_at(owner):
        return all_kv.at[:, pl.ds(pl.multiple_of(owner * tokens, tokens), tokens), :]

    def block_at(owner):
        return out.at[me_dp, owner]

    kv_hops = [hop(local, kv_at, step, 1, ks, kr) for step in range(rows - 1)]
    hops = [
        (hop(shard, block_at, step, 1, zs, zr), hop(shard, block_at, step, -1, ys, yr))
        for step in range(rows - 1)
    ]

    def launch(item):
        pl.when(item[1])(item[0].start)

    def receive(item):
        pl.when(item[2])(item[0].wait_recv)

    def far_copy(owner, block, slot, far):
        return pltpu.make_async_remote_copy(
            src_ref=block,
            dst_ref=out.at[me_dp, owner],
            send_sem=xs.at[slot, far - 1],
            recv_sem=xr.at[slot, far - 1],
            device_id={"dp": place("dp", far)},
            device_id_type=pl.DeviceIdType.MESH,
        )

    across = []

    def send_across(slot, owner, block, valid):
        for far in range(1, groups):
            copy = far_copy(owner, block, slot, far)
            pl.when(valid)(copy.start)
            across.append((copy, valid))

    def step_rest(step):
        for side, item in enumerate(hops[step]):
            receive(item)
            send_across(1 + 2 * step + side, item[3], block_at(item[3]), item[2])

    launch(kv_hops[0])
    for item in hops[0]:
        launch(item)
    send_across(0, me_ctx, shard, me_ctx >= 0)
    all_kv[:, pl.ds(start, tokens), :] = local[...]
    out[me_dp, me_ctx] = shard[...]
    for block in range(1, rows):

        @pl.when(block > me_ctx)
        def _(block=block):
            later = all_kv.at[:, block * tokens : (block + 1) * tokens, :]
            later[...] = jnp.zeros(later.shape, LOW)

    for step in range(1, rows - 1):
        receive(kv_hops[step - 1])
        launch(kv_hops[step])
        step_rest(step - 1)
        for item in hops[step]:
            launch(item)
    receive(kv_hops[rows - 2])
    for one in range(batch):
        allowed = allowed_pairs(segment_row[one], segment_column[one])
        total[...] = jnp.zeros_like(total)

        def one_head(head, carry):
            masked = query[one] * head_lanes(key_width, 0, head).astype(LOW)
            probs = softmax_of(masked, all_kv[one, :, :key_width], allowed)
            part = dot(probs.astype(LOW), all_kv[one, :, lead:], 1, 0)
            total[...] += part * head_lanes(value_width, width - lead, head)
            return carry

        lax.fori_loop(0, width // HD, one_head, 0)
        mixed[one] = total[...].astype(LOW)
        if one == 0:
            step_rest(rows - 2)
    for copy, valid in across:
        pl.when(valid)(copy.wait)
    for item in kv_hops + [item for pair in hops for item in pair]:
        pl.when(item[1])(item[0].wait_send)


def attend(width, local, query, segment_row, segment_column, shard):
    groups, rows = lax.axis_size("dp"), lax.axis_size("ctx")
    batch, tokens = local.shape[:2]
    value_width = 2 * width - width // 128 * 128
    dma = pltpu.SemaphoreType.DMA
    return pl.pallas_call(
        functools.partial(attend_kernel, width),
        out_shape=(
            jax.ShapeDtypeStruct((batch, rows * tokens, 2 * width), LOW),
            jax.ShapeDtypeStruct((batch, tokens, value_width), LOW),
            jax.ShapeDtypeStruct((groups, rows) + shard.shape, LOW),
        ),
        in_specs=whole(5),
        out_specs=tuple(whole(3)),
        scratch_shapes=[pltpu.VMEM((tokens, value_width), F32)]
        + [dma((rows - 1,))] * 6
        + [dma((2 * rows - 1, groups - 1))] * 2,
        compiler_params=params(2),
    )(local, query, segment_row, segment_column, shard)


def attend_back_kernel(
    width, mixed_grad, query, all_kv, segment_row, segment_column, g0, g1, g2,
    down_part, middle, table,
    kv_grad, query_grad, value_sum, sum0, sum1, sum2, result,
    total, parts, landing, dp0, dp1, dp2, pass0, pass1, pass2, ctx0, ctx1, ctx2,
    land_down, ks, kr, xs, xr, zs, zr, ds, dr,
):
    groups, rows = lax.axis_size("dp"), lax.axis_size("ctx")
    me_dp, me_ctx = lax.axis_index("dp"), lax.axis_index("ctx")
    batch, tokens = kv_grad.shape[:2]
    key_width, value_width = query.shape[2], mixed_grad.shape[2]
    lead = 2 * width - value_width
    weights = (
        (g0, sum0, dp0, pass0, ctx0),
        (g1, sum1, dp1, pass1, ctx1),
        (g2, sum2, dp2, pass2, ctx2),
    )
    order = list(range(1, rows)) + [0]
    greet(("dp", "ctx", "tensor"))
    down_copies = start_shares(down_part, land_down, ds, dr)
    across, along = {}, []
    for step in order:
        for at, (grads, _, land_dp, _, _) in enumerate(weights):
            for far in range(1, groups):
                peer = place("dp", far)
                across[step, at, far] = push(
                    grads.at[peer, place("ctx", step)],
                    land_dp.at[step, far - 1],
                    xs.at[at, step, far - 1],
                    xr.at[at, step, far - 1],
                    {"dp": peer},
                )
    value_sum[...] = jnp.zeros_like(value_sum)
    kv_copies = []

    def pass_block(step):
        owner = place("ctx", step)
        for at, (grads, summed, land_dp, pass_on, land_ctx) in enumerate(weights):
            for far in range(1, groups):
                across[step, at, far].wait()
            value = grads[me_dp, owner].astype(F32)
            for far in range(1, groups):
                value = value + land_dp[step, far - 1].astype(F32)
            if step == 0:
                summed[...] = value
            else:
                pass_on[step - 1] = value.astype(LOW)
                along.append(
                    push(
                        pass_on.at[step - 1],
                        land_ctx.at[step - 1],
                        zs.at[at, step - 1],
                        zr.at[at, step - 1],
                        {"ctx": owner},
                    )
                )

    pass_block(order[0])
    for one in range(batch):
        allowed = allowed_pairs(segment_row[one], segment_column[one])
        total[...] = jnp.zeros_like(total)
        query_grad[one] = jnp.zeros(query_grad.shape[1:], F32)

        def one_head(head, carry):
            lanes = head_lanes(key_width, 0, head)
            masked = query[one] * lanes.astype(LOW)
            keys = all_kv[one, :, :key_width]
            probs = softmax_of(masked, keys, allowed)
            masked_grad = mixed_grad[one] * head_lanes(value_width, width - lead, head).astype(LOW)
            prob_grad = dot(masked_grad, all_kv[one, :, lead:], 1, 1)
            delta = jnp.sum(prob_grad * probs, axis=-1, keepdims=True)
            score_grad = (probs * (prob_grad - delta) * HD ** (-0.5)).astype(LOW)
            query_grad[one] += dot(score_grad, keys, 1, 0) * lanes
            total[:, :key_width] += dot(score_grad, masked, 0, 0)
            total[:, lead:] += dot(probs.astype(LOW), masked_grad, 0, 0)
            return carry

        lax.fori_loop(0, width // HD, one_head, 0)
        value_sum[0:1] += jnp.sum(total[...], axis=0, keepdims=True)
        parts[one] = total[...].astype(LOW)
        for step in range(1, rows):
            peer = place("ctx", step)
            kv_copies.append(
                push(
                    parts.at[one, pl.ds(pl.multiple_of(peer * tokens, tokens), tokens), :],
                    landing.at[step - 1, one],
                    ks.at[one, step - 1],
                    kr.at[one, step - 1],
                    {"ctx": peer},
                )
            )
        if one == 0:
            for step in order[1:]:
                pass_block(step)
    for copy in down_copies:
        copy.wait()
    share = middle.shape[1]
    start = pl.multiple_of(lax.axis_index("tensor") * share, share)
    value = sum_shares(down_part, land_down, start)
    result[...] = (middle[...] + value + table[7:8][None]).astype(LOW)
    start = pl.multiple_of(me_ctx * tokens, tokens)
    for copy in kv_copies:
        copy.wait()
    value = parts[:, pl.ds(start, tokens), :].astype(F32)
    for step in range(1, rows):
        value = value + landing[step - 1].astype(F32)
    kv_grad[...] = value.astype(LOW)
    for copy in along:
        copy.wait()
    for _, summed, _, _, land_ctx in weights:
        value = summed[...]
        for step in range(1, rows):
            value = value + land_ctx[step - 1].astype(F32)
        summed[...] = value


def attend_back(
    width, mixed_grad, query, all_kv, segment_row, segment_column, weight_grads, down_part, middle, table
):
    groups, rows = lax.axis_size("dp"), lax.axis_size("ctx")
    batch, tokens, key_width = query.shape
    length = rows * tokens
    blocks = [grads.shape[2:] for grads in weight_grads]
    dma = pltpu.SemaphoreType.DMA
    return pl.pallas_call(
        functools.partial(attend_back_kernel, width),
        out_shape=(
            jax.ShapeDtypeStruct((batch, tokens, 2 * width), LOW),
            jax.ShapeDtypeStruct(query.shape, F32),
            jax.ShapeDtypeStruct((8, 2 * width), F32),
        )
        + tuple(jax.ShapeDtypeStruct(block, F32) for block in blocks)
        + (jax.ShapeDtypeStruct(middle.shape, LOW),),
        in_specs=whole(11),
        out_specs=tuple(whole(7)),
        scratch_shapes=[
            pltpu.VMEM((length, 2 * width), F32),
            pltpu.VMEM((batch, length, 2 * width), LOW),
            pltpu.VMEM((rows - 1, batch, tokens, 2 * width), LOW),
        ]
        + [pltpu.VMEM((rows, groups - 1) + block, LOW) for block in blocks]
        + [pltpu.VMEM((rows - 1,) + block, LOW) for block in blocks] * 2
        + [pltpu.VMEM((lax.axis_size("tensor") - 1,) + middle.shape, LOW)]
        + [dma((batch, rows - 1))] * 2
        + [dma((3, rows, groups - 1))] * 2
        + [dma((3, rows - 1))] * 2
        + [dma((lax.axis_size("tensor") - 1,))] * 2,
        compiler_params=params(3),
    )(
        mixed_grad, query, all_kv, segment_row, segment_column, *weight_grads,
        down_part, middle, table,
    )


def start_shares(parts, landing, sends, receives):
    share = landing.shape[2]
    copies = []
    for step in range(1, lax.axis_size("tensor")):
        peer = place("tensor", step)
        copies.append(
            push(
                parts.at[:, pl.ds(pl.multiple_of(peer * share, share), share), :],
                landing.at[step - 1],
                sends.at[step - 1],
                receives.at[step - 1],
                {"tensor": peer},
            )
        )
    return copies


def sum_shares(parts, landing, start):
    total = parts[:, pl.ds(start, landing.shape[2]), :].astype(F32)
    for step in range(landing.shape[0]):
        total = total + landing[step].astype(F32)
    return total


def spread_shares(out, start, share, sends, receives, meanwhile):
    ways = lax.axis_size("tensor")
    index = lax.axis_index("tensor")

    def send(block, slot, peer):
        rows = out.at[:, pl.ds(pl.multiple_of(block * share, share), share), :]
        return push(rows, rows, sends.at[slot], receives.at[slot], {"tensor": peer})

    if ways == 4:
        far = lax.rem(index + 2, 4)
        near = index + 1 - 2 * lax.rem(index, 2)
        copies = [send(index, 0, far), send(index, 1, near)]
        meanwhile()
        copies[0].wait_recv()
        copies.append(send(far, 2, near))
    else:
        copies = [send(index, step - 1, place("tensor", step)) for step in range(1, ways)]
        meanwhile()
        copies[0].wait_recv()
    for copy in copies[1:]:
        copy.wait_recv()
    for copy in copies:
        copy.wait_send()


def forward_share_kernel(parts, inputs, table, out, middle, landing, s0, r0, s1, r1):
    share = middle.shape[1]
    start = pl.multiple_of(lax.axis_index("tensor") * share, share)
    greet(("tensor",))
    copies = start_shares(parts, landing, s0, r0)
    for copy in copies:
        copy.wait()
    total = sum_shares(parts, landing, start)
    values = inputs[:, pl.ds(start, share), :].astype(F32) + total + table[4:5][None]
    middle[...] = values
    unit, scale = unit_norm(values)
    out[:, pl.ds(start, share), :] = (unit * table[5:6][None] + table[6:7][None]).astype(LOW)
    spread_shares(out, start, share, s1, r1, lambda: None)


def backward_share_kernel(parts, back, middle, table, out, grad, sums, landing, s0, r0, s1, r1):
    share = middle.shape[1]
    start = pl.multiple_of(lax.axis_index("tensor") * share, share)
    greet(("tensor",))
    copies = start_shares(parts, landing, s0, r0)
    back_rows = back[:, pl.ds(start, share), :].astype(F32)
    unit, scale = unit_norm(middle[...])
    for copy in copies:
        copy.wait()
    total = sum_shares(parts, landing, start)
    values = back_rows + norm_back(total, table[5:6][None], unit, scale)
    grad[...] = values
    out[:, pl.ds(start, share), :] = values.astype(LOW)

    def add_rows():
        sums[...] = jnp.zeros_like(sums)
        for row, term in enumerate((values, total * unit, total, back_rows)):
            sums[row : row + 1] = jnp.sum(jnp.sum(term, axis=0), axis=0, keepdims=True)

    spread_shares(out, start, share, s1, r1, add_rows)


def share_scratch(parts, copies):
    ways = lax.axis_size("tensor")
    batch, tokens, model = parts.shape
    return [pltpu.VMEM((ways - 1, batch, tokens // ways, model), LOW)] + [
        pltpu.SemaphoreType.DMA((ways - 1,))
    ] * copies


def forward_share(parts, inputs, table):
    ways = lax.axis_size("tensor")
    batch, tokens, model = parts.shape
    return pl.pallas_call(
        forward_share_kernel,
        out_shape=(
            jax.ShapeDtypeStruct(parts.shape, LOW),
            jax.ShapeDtypeStruct((batch, tokens // ways, model), F32),
        ),
        in_specs=whole(3),
        out_specs=tuple(whole(2)),
        scratch_shapes=share_scratch(parts, 4),
        compiler_params=params(4),
    )(parts, inputs, table)


def backward_share(parts, back, middle, table):
    return pl.pallas_call(
        backward_share_kernel,
        out_shape=(
            jax.ShapeDtypeStruct(parts.shape, LOW),
            jax.ShapeDtypeStruct(middle.shape, F32),
            jax.ShapeDtypeStruct((8, parts.shape[2]), F32),
        ),
        in_specs=whole(4),
        out_specs=tuple(whole(3)),
        scratch_shapes=share_scratch(parts, 4),
        compiler_params=params(5),
    )(parts, back, middle, table)


def final_kernel(
    grads, first_part, inputs, middle_grad, table, owned,
    grad_sum, input_grad, vector_sum,
    land_dp, pass_on, land_ctx, land_first, land_t, land_c, land_d,
    xs, xr, zs, zr, fs, fr, ts, tr, cs, cr, es, er,
):
    groups, rows = lax.axis_size("dp"), lax.axis_size("ctx")
    me_dp, me_ctx = lax.axis_index("dp"), lax.axis_index("ctx")
    share = middle_grad.shape[1]
    start = pl.multiple_of(lax.axis_index("tensor") * share, share)
    greet(("dp", "ctx", "tensor"))
    order = list(range(1, rows)) + [0]
    across = {}
    for step in order:
        for far in range(1, groups):
            peer = place("dp", far)
            across[step, far] = push(
                grads.at[peer, place("ctx", step)],
                land_dp.at[step, far - 1],
                xs.at[step, far - 1],
                xr.at[step, far - 1],
                {"dp": peer},
            )
    first_copies = start_shares(first_part, land_first, fs, fr)

    along = []
    for step in order:
        owner = place("ctx", step)
        for far in range(1, groups):
            across[step, far].wait()
        total = grads[me_dp, owner].astype(F32)
        for far in range(1, groups):
            total = total + land_dp[step, far - 1].astype(F32)
        if step == 0:
            grad_sum[...] = total
        else:
            pass_on[step - 1] = total.astype(LOW)
            along.append(
                push(
                    pass_on.at[step - 1],
                    land_ctx.at[step - 1],
                    zs.at[step - 1],
                    zr.at[step - 1],
                    {"ctx": owner},
                )
            )

    for copy in first_copies:
        copy.wait()
    total = sum_shares(first_part, land_first, start)
    unit, scale = unit_norm(inputs[:, pl.ds(start, share), :].astype(F32))
    input_grad[...] = middle_grad[...] + norm_back(total, table[0:1][None], unit, scale)
    vector_sum[...] = owned[...]
    vector_sum[0:1] = jnp.sum(jnp.sum(total * unit, axis=0), axis=0, keepdims=True)
    vector_sum[1:2] = jnp.sum(jnp.sum(total, axis=0), axis=0, keepdims=True)
    for axis, land, sends, receives in (
        ("tensor", land_t, ts, tr),
        ("ctx", land_c, cs, cr),
        ("dp", land_d, es, er),
    ):
        copies = [
            push(
                vector_sum,
                land.at[step - 1],
                sends.at[step - 1],
                receives.at[step - 1],
                {axis: place(axis, step)},
            )
            for step in range(1, lax.axis_size(axis))
        ]
        for copy in copies:
            copy.wait()
        summed = vector_sum[...]
        for step in range(1, lax.axis_size(axis)):
            summed = summed + land[step - 1]
        vector_sum[...] = summed

    for copy in along:
        copy.wait()
    summed = grad_sum[...]
    for step in range(1, rows):
        summed = summed + land_ctx[step - 1].astype(F32)
    grad_sum[...] = summed


def finish(grads, first_part, inputs, middle_grad, table, owned):
    groups, rows = lax.axis_size("dp"), lax.axis_size("ctx")
    ways = lax.axis_size("tensor")
    block = grads.shape[2:]
    dma = pltpu.SemaphoreType.DMA
    land = pltpu.VMEM((ways - 1,) + middle_grad.shape, LOW)
    pairs = ((rows, groups - 1), (rows - 1,), (ways - 1,))
    pairs += ((ways - 1,), (rows - 1,), (groups - 1,))
    return pl.pallas_call(
        final_kernel,
        out_shape=(
            jax.ShapeDtypeStruct(block, F32),
            jax.ShapeDtypeStruct(middle_grad.shape, F32),
            jax.ShapeDtypeStruct(owned.shape, F32),
        ),
        in_specs=whole(6),
        out_specs=tuple(whole(3)),
        scratch_shapes=[
            pltpu.VMEM((rows, groups - 1) + block, LOW),
            pltpu.VMEM((rows - 1,) + block, LOW),
            pltpu.VMEM((rows - 1,) + block, LOW),
            land,
            pltpu.VMEM((ways - 1,) + owned.shape, F32),
            pltpu.VMEM((rows - 1,) + owned.shape, F32),
            pltpu.VMEM((groups - 1,) + owned.shape, F32),
        ]
        + [dma(shape) for shape in pairs for _ in range(2)],
        compiler_params=params(6),
    )(grads, first_part, inputs, middle_grad, table, owned)


def on_device(
    hidden_in,
    cotangent,
    segment_ids,
    qkv_weight,
    qkv_first,
    qkv_second,
    out_weight,
    out_first,
    out_second,
    up_weight,
    up_first,
    up_second,
    down_weight,
    down_first,
    down_second,
    vectors,
    vectors_first,
    vectors_second,
):
    batch, tokens, model = hidden_in.shape
    width = qkv_weight.shape[2]
    units = up_weight.shape[1]
    rows_all = batch * tokens
    tensor_index = lax.axis_index("tensor")

    shard = jnp.concatenate([qkv_weight[0], qkv_weight[1], qkv_weight[2]], axis=1).astype(LOW)
    rest_shard = jnp.concatenate([up_weight, down_weight.T, out_weight.T], axis=1).astype(LOW)
    table_rows, part = vectors.shape
    pad_rows = -table_rows % 16
    small = jnp.pad(vectors.astype(LOW), ((0, pad_rows), (0, -part % 128)))
    gathered, small_all = gather_weights(shard, small)
    proj = gathered.reshape(model, shard.shape[1])
    small_all = small_all.reshape((-1,) + small.shape)[:, :, :part]
    table = small_all.transpose(1, 0, 2).reshape(small.shape[0], model).astype(F32)

    unit_first, _ = unit_norm(hidden_in.astype(F32))
    first_norm = (unit_first * table[0] + table[1]).astype(LOW).reshape(rows_all, model)
    projected = dot(first_norm, proj, 1, 0)
    query_bias = lax.dynamic_slice_in_dim(table[2], tensor_index * width, width)
    value_bias = lax.dynamic_slice_in_dim(table[3], tensor_index * width, width)
    query = (projected[:, :width] + query_bias).astype(LOW).reshape(batch, tokens, width)
    local_kv = (
        jnp.concatenate(
            [projected[:, width : 2 * width], projected[:, 2 * width :] + value_bias], axis=1
        )
        .astype(LOW)
        .reshape(batch, tokens, 2 * width)
    )
    lead = width // 128 * 128
    query = jnp.pad(query, ((0, 0), (0, 0), (0, -width % 128)))
    segment_row = segment_ids[:, None, :]
    segment_column = lax.dynamic_slice_in_dim(
        segment_ids, lax.axis_index("ctx") * tokens, tokens, 1
    )[:, :, None]
    all_kv, mixed, rest = attend(width, local_kv, query, segment_row, segment_column, rest_shard)
    rest = rest.reshape(model, rest_shard.shape[1])
    up = rest[:, :units]
    down_turned = rest[:, units : 2 * units]
    out_turned = rest[:, 2 * units :]
    mixed = mixed[:, :, width - lead :].reshape(rows_all, width)

    attn_part = dot(mixed, out_turned, 1, 1).astype(LOW).reshape(batch, tokens, model)
    second_norm, middle = forward_share(attn_part, hidden_in, table)
    second_norm = second_norm.reshape(rows_all, model)
    unit_bias = lax.dynamic_slice_in_dim(
        table[8:table_rows].reshape(-1), tensor_index * units, units
    )
    hidden = dot(second_norm, up, 1, 0) + unit_bias
    gelu_value, gelu_pull = jax.vjp(jax.nn.gelu, hidden)
    active = gelu_value.astype(LOW)
    down_part = dot(active, down_turned, 1, 1).astype(LOW).reshape(batch, tokens, model)

    back = cotangent.reshape(rows_all, model)
    hidden_grad = gelu_pull(dot(back, down_turned, 1, 0))[0]
    hidden_low = hidden_grad.astype(LOW)
    second_part = dot(hidden_low, up, 1, 1).astype(LOW).reshape(batch, tokens, model)
    middle_low, middle_grad, late_rows = backward_share(second_part, cotangent, middle, table)
    grad_down = dot(back, active, 0, 0)
    grad_up = dot(second_norm, hidden_low, 0, 0)

    middle_low = middle_low.reshape(rows_all, model)
    mixed_grad = dot(middle_low, out_turned, 1, 0).astype(LOW).reshape(batch, tokens, width)
    mixed_grad = jnp.pad(mixed_grad, ((0, 0), (0, 0), (width - lead, 0)))
    grad_out = dot(middle_low, mixed, 0, 0)
    blocks = (lax.axis_size("dp"), lax.axis_size("ctx"), shard.shape[0])
    weight_grads = [
        grads.astype(LOW).reshape(blocks + (-1,)) for grads in (grad_up, grad_down, grad_out)
    ]
    kv_grad, query_grad, value_sum, up_sum, down_sum, out_sum, result = attend_back(
        width, mixed_grad, query, all_kv, segment_row, segment_column, weight_grads,
        down_part, middle, table,
    )
    query_grad = query_grad[:, :, :width]
    stacked = jnp.concatenate([query_grad.astype(LOW), kv_grad], axis=2).reshape(
        rows_all, 3 * width
    )
    first_part = dot(stacked, proj, 1, 1).astype(LOW).reshape(batch, tokens, model)
    grad_qkv = dot(first_norm, stacked, 0, 0)
    grads = grad_qkv.astype(LOW).reshape(blocks + (-1,))

    owned = jnp.zeros((small.shape[0] * model,), F32)
    owned = lax.dynamic_update_slice(
        owned, jnp.sum(query_grad, axis=(0, 1)), (2 * model + tensor_index * width,)
    )
    owned = lax.dynamic_update_slice(
        owned, value_sum[0, width:], (3 * model + tensor_index * width,)
    )
    owned = lax.dynamic_update_slice(owned, late_rows[:4].reshape(-1), (4 * model,))
    owned = lax.dynamic_update_slice(
        owned, jnp.sum(hidden_grad, axis=0), (8 * model + tensor_index * units,)
    ).reshape(small.shape[0], model)

    grad_sum, input_grad, vector_sum = finish(
        grads, first_part, hidden_in, middle_grad, table, owned
    )
    grad_vectors = lax.dynamic_slice_in_dim(
        vector_sum[:table_rows],
        (lax.axis_index("dp") * lax.axis_size("ctx") + lax.axis_index("ctx")) * part,
        part,
        1,
    )
    qkv_sum = jnp.stack([grad_sum[:, at * width : (at + 1) * width] for at in range(3)])
    out_sum = out_sum.T
    down_sum = down_sum.T
    return (
        result,
        input_grad,
        *adamw(qkv_weight, qkv_first, qkv_second, qkv_sum, rate_qkv, weight_decay),
        *adamw(out_weight, out_first, out_second, out_sum, rate_out, weight_decay),
        *adamw(up_weight, up_first, up_second, up_sum, rate_up, weight_decay),
        *adamw(down_weight, down_first, down_second, down_sum, rate_down, weight_decay),
        *adamw(vectors, vectors_first, vectors_second, grad_vectors, rate_vectors, 0.0),
    )


def solution(mesh):
    tokens = P("dp", "ctx", None)
    shares = P("dp", ("ctx", "tensor"), None)
    by_row = P(("dp", "ctx"), "tensor")
    by_column = P("tensor", ("dp", "ctx"))
    stacked = P(None, ("dp", "ctx"), "tensor")
    narrow = P(None, ("dp", "ctx"))
    states = (stacked,) * 3 + (by_column,) * 3 + (by_row,) * 3 + (by_column,) * 3 + (narrow,) * 3
    return jax.shard_map(
        on_device,
        mesh=mesh,
        in_specs=(tokens, tokens, P("dp", None)) + states,
        out_specs=(shares, shares) + states,
        check_vma=False,
    )
```
